32 devices in a mesh: sect: 2 (over core), dom: 16 (over z, y, x).
Axes of the slice: x: 2, y: 2, z: 4, core: 2. Of those that a mesh axis runs over, the one named last changes fastest.
Arguments:
- forcing: float32 [2, 4096, 2048], P('sect', 'dom'), may hold values from -6 to 6
- coefficient: float32 [2, 4096, 2048], P('sect', 'dom'), may hold values from 0.05 to 2
- cell_mask: int32 [2, 4096, 2048], P('sect', 'dom'), may hold values 0 or 1
- remap_weight: float32 [2, 1024, 2048], P('sect', 'dom'), may hold values from 0.1 to 1
- remap_index: int32 [2, 1024, 2048], P('sect', 'dom'), may hold values from 0 to 2047
- link_source: int32 [2, 1024], P('sect', 'dom'), may hold values from 0 to 255
- link_target: int32 [2, 1024], P('sect', 'dom'), may hold values from 0 to 4095, as said below
Outputs:
- coupled: float32 [2, 4096, 2048], P('sect', 'dom')
The draws below stay inside these ranges and needn't reach their ends.
Inputs may be any that keep to these rules, and one draw needn't show every extreme that they name: `link_target`: within each section, the 64 entries of a partition name exactly 16 distinct partitions of the other section, 4 entries each, in any order; one partition of the other section, drawn anew, receives 4 entries from every partition.
All inputs are finite; a program needn't handle non-finite values. No bound on the sum of `cell_mask` on one device may be relied on, other than what follows from the above.
Results may differ from the reference program's by a relative error of at most 0.000071.
Values sent between devices are 32-bit elements; how exact they have to be, the bound alone decides.
No kernel may reach another device: no remote copies, remote signals or barrier semaphores. Data moves between devices by JAX's collectives and lax.ppermute only.
A program may use at most 64 MiB of HBM per device.

```python
import math
import jax
import jax.numpy as jnp

ROWS = 256
CELLS = 2048
ENTRIES = 64
CAP = 4
SWEEPS = 20
GRID_ROWS = 4096
ALL_ENTRIES = 1024
N_DOM = 16


def draw_link_target(key, part):
    key = jax.random.fold_in(key, 11)

    def one_section(section_key):
        hot_key, rest_key = jax.random.split(section_key)
        hottest = jax.random.randint(hot_key, (), 0, N_DOM).astype(jnp.int32)

        def one_holder(holder_key):
            first_key, second_key, third_key = jax.random.split(holder_key, 3)
            others = (hottest + 1 + jax.random.permutation(first_key, N_DOM - 1).astype(jnp.int32)) % N_DOM
            ordering = jnp.concatenate([hottest[None], others])
            targets = ordering[jnp.arange(ENTRIES) // CAP]
            within = jax.random.randint(second_key, (ENTRIES,), 0, ROWS).astype(jnp.int32)
            shuffle = jax.random.permutation(third_key, ENTRIES)
            return (targets * ROWS + within)[shuffle]
        return jax.vmap(one_holder)(jax.random.split(rest_key, N_DOM)).reshape(N_DOM * ENTRIES)
    return jax.vmap(one_section)(jax.random.split(key, 2)).astype(jnp.int32)


def place_ends(array, key, low, largest):
    longest = array.shape.index(max(array.shape))
    spots = []
    for shift in (0, 1):
        where = [jax.random.randint(jax.random.fold_in(key, axis), (), 0, length) for axis, length in enumerate(array.shape)]
        where[longest] = (where[longest] + shift) % array.shape[longest]
        spots.append(tuple(where))
    return array.at[spots[0]].set(low).at[spots[1]].set(largest)


def block_levels(rng, dims, cuts, smallest, high):
    factor_of = 1.0
    for position, blocks in cuts:
        heights = jax.random.uniform(jax.random.fold_in(jax.random.fold_in(rng, 6), position), (blocks,), jnp.float32, smallest / len(cuts), high / len(cuts))
        factor_of = factor_of * jnp.repeat(jnp.exp(heights), dims[position] // blocks).reshape((-1,) + (1,) * (len(dims) - 1 - position))
    return factor_of


def centred(stream_key, dims, spread, reach, cuts=(), held_as=jnp.bfloat16):
    entries = jax.random.normal(stream_key, dims, jnp.float32) * spread
    if len(cuts) > 0:
        entries = block_levels(stream_key, dims, cuts, -0.22, 0.18) * entries
    return jnp.clip(entries, min=-reach, max=reach).astype(held_as)


def setup_inputs(seed: int = 0) -> dict:
    arg_keys = jax.random.split(jax.random.key(seed), 8)
    return {
        "forcing": centred(arg_keys[0], (2, GRID_ROWS, CELLS), 1.0, 6.0, ((0, 2), (1, 16)), jnp.float32),
        "coefficient": jnp.clip(jnp.exp(math.log(2.0) - 3.6888794 * jax.random.uniform(arg_keys[1], (2, GRID_ROWS, CELLS), jnp.float32) ** block_levels(arg_keys[1], (2, GRID_ROWS, CELLS), ((0, 2), (1, 16)), -0.2, 0.2)), 0.05, 2.0),
        "cell_mask": place_ends((jax.random.randint(arg_keys[2], (2, GRID_ROWS, CELLS), 0, 8) < 7).astype(jnp.int32), jax.random.fold_in(arg_keys[2], 1), 0, 1),
        "remap_weight": jnp.clip(0.1 + 0.9 * jax.random.uniform(arg_keys[3], (2, ALL_ENTRIES, CELLS), jnp.float32) ** block_levels(arg_keys[3], (2, ALL_ENTRIES, CELLS), ((0, 2), (1, 16)), -0.2, 0.2), 0.1, 1.0),
        "remap_index": place_ends(jax.random.randint(arg_keys[4], (2, ALL_ENTRIES, CELLS), 0, CELLS), jax.random.fold_in(arg_keys[4], 1), 0, CELLS - 1).astype(jnp.int32),
        "link_source": place_ends(jax.random.randint(arg_keys[5], (2, ALL_ENTRIES), 0, ROWS), jax.random.fold_in(arg_keys[5], 1), 0, ROWS - 1).astype(jnp.int32),
        "link_target": draw_link_target(jax.random.fold_in(arg_keys[7], 71), 0),
    }


def relax(padded, stress, friction, cut_mask):
    middle = padded[1:-1]
    vertical = padded[:-2] + padded[2:]
    left_side = jnp.pad(middle, ((0, 0), (1, 0)))[:, :-1]
    right_side = jnp.pad(middle, ((0, 0), (0, 1)))[:, 1:]
    return cut_mask * (stress + 1.0 * vertical + 0.25 * (left_side + right_side)) / (2.5 + friction)


def reference(forcing, coefficient, cell_mask, remap_weight, remap_index, link_source, link_target):
    masks = cell_mask.astype(jnp.float32)
    holder = (jnp.arange(ALL_ENTRIES, dtype=jnp.int32) // ENTRIES) * ROWS
    melt_flux = masks[0] * coefficient[0] * forcing[0]
    gathered = jnp.take_along_axis(melt_flux[holder + link_source[0]], remap_index[0], axis=1)
    sent_melt = remap_weight[0] * gathered
    ice_melt = jnp.zeros((GRID_ROWS, CELLS), jnp.float32).at[link_target[0]].add(sent_melt)
    velocity = jnp.zeros((GRID_ROWS, CELLS), jnp.float32)
    for sweep_index in range(SWEEPS):
        velocity = relax(jnp.pad(velocity, ((1, 1), (0, 0))), forcing[1], coefficient[1], masks[1])
    east_side = jnp.pad(velocity, ((0, 0), (0, 1)))[:, 1:]
    west_side = jnp.pad(velocity, ((0, 0), (1, 0)))[:, :-1]
    thickness_change = masks[1] * (-ice_melt - 0.5 * (east_side - west_side))
    values = remap_weight[1] * thickness_change[holder + link_source[1]]
    entry_rows = jnp.arange(ALL_ENTRIES, dtype=jnp.int32)[:, None]
    back = jnp.zeros((ALL_ENTRIES, CELLS), jnp.float32).at[entry_rows, remap_index[1]].add(values)
    returned = jnp.zeros((GRID_ROWS, CELLS), jnp.float32).at[link_target[1]].add(back)
    return jnp.stack([masks[0] * returned, velocity])
```

```python
import functools

import jax
import jax.numpy as jnp
from jax import lax
from jax.experimental import pallas as pl
from jax.experimental.pallas import tpu as pltpu
from jax.sharding import PartitionSpec as P

CAP = 4
SWEEPS = 20
LANES = 128
SUB = 8
HALO = 24
BITS = 2

F32 = jnp.float32
BF16 = jnp.bfloat16
ANY = pl.BlockSpec(memory_space=pl.ANY)
HBM = pl.BlockSpec(memory_space=pltpu.HBM)
VMEM = pl.BlockSpec(memory_space=pltpu.VMEM)
SMEM = pl.BlockSpec(memory_space=pltpu.SMEM)


def params(mib):
    return pltpu.CompilerParams(vmem_limit_bytes=mib * 2**20)


def cost(microseconds):
    return pl.CostEstimate(flops=0, bytes_accessed=int(microseconds * 3.0e6), transcendentals=0)


def pieces(x, count):
    out = []
    for _ in range(count - 1):
        head = x.astype(BF16)
        out.append(head)
        x = x - head.astype(F32)
    out.append(x.astype(BF16))
    return out


def one_hot_dot(picker, table, count):
    total = None
    for piece in pieces(table, count):
        part = jnp.dot(picker, piece, preferred_element_type=F32)
        total = part if total is None else total + part
    return total


def halo_kernel(sec_ref, f_hbm, c_hbm, m_hbm, last_ref, first_ref, stress, fric, mask, sems):
    height = f_hbm.shape[0]

    @pl.when(sec_ref[0] == 1)
    def _():
        copies = []
        for k, start in enumerate((height - HALO, 0)):
            for q, (src, dst) in enumerate(((f_hbm, stress), (c_hbm, fric), (m_hbm, mask))):
                copy = pltpu.make_async_copy(src.at[pl.ds(start, HALO)], dst.at[k], sems.at[3 * k + q])
                copy.start()
                copies.append(copy)
        for copy in copies:
            copy.wait()
        for k, ref in enumerate((last_ref, first_ref)):
            ref[:HALO, :] = stress[k]
            ref[HALO:, :] = mask[k].astype(F32) / (2.5 + fric[k])


def halo_rows(section, forcing, coefficient, mask):
    cells = forcing.shape[1]
    out = jax.ShapeDtypeStruct((2 * HALO, cells), F32)
    return pl.pallas_call(
        halo_kernel,
        out_shape=(out, out),
        in_specs=[SMEM, HBM, HBM, HBM],
        out_specs=(VMEM, VMEM),
        scratch_shapes=[
            pltpu.VMEM((2, HALO, cells), F32),
            pltpu.VMEM((2, HALO, cells), F32),
            pltpu.VMEM((2, HALO, cells), jnp.int32),
            pltpu.SemaphoreType.DMA((6,)),
        ],
        compiler_params=params(16),
        cost_estimate=cost(2),
        name="halo_rows",
    )(section, forcing, coefficient, mask)


def prepare_kernel(
    zero_fill, sec_ref, src_ref, tgt_ref, tie_ref, f_hbm, c_hbm, m_hbm, w_hbm, ix_hbm,
    first_ref, second_ref, slot_ref, list_ref, a_ref, b_ref, gain_ref,
    stress, ratio, fric, mask, wbuf, ixbuf, m_rows, melt, sent, rank, filled, sems,
):
    del tie_ref
    height, cells = f_hbm.shape
    entries = w_hbm.shape[0]
    cols = cells // LANES
    block = 2 * cols + SUB
    partitions = rank.shape[0]
    padded = height + 2 * HALO
    rows = padded // SUB
    ocean, ice = sec_ref[0] == 0, sec_ref[0] == 1

    copies = []

    def fetch(src, dst):
        copy = pltpu.make_async_copy(src, dst, sems.at[len(copies)])
        copy.start()
        copies.append(copy)

    for j in range(cols):
        s = pl.ds(j * LANES, LANES)
        fetch(c_hbm.at[:, s], fric.at[j])
        fetch(m_hbm.at[:, s], mask.at[j])
        fetch(f_hbm.at[:, s], stress.at[j, pl.ds(HALO, height)])
    fetch(w_hbm, wbuf)
    fetch(ix_hbm, ixbuf)

    if zero_fill:
        first_ref[...] = jnp.full(first_ref.shape, -1.0, F32)
        second_ref[...] = jnp.zeros_like(second_ref)
    for p in range(partitions):
        rank[p] = 0
        if zero_fill:
            first_ref[p * block : p * block + 2 * cols, :] = jnp.zeros((2 * cols, LANES), F32)
        else:
            second_ref[p * block + 2 * cols : (p + 1) * block, :] = jnp.zeros((SUB, LANES), F32)
    filled[0] = 0
    filled[1] = 0
    if zero_fill:
        for p in range(partitions):
            second_ref[p * block + 2 * cols : (p + 1) * block, :] = jnp.zeros((SUB, LANES), F32)

    def assign(e, carry):
        target = tgt_ref[e]
        p = lax.div(target, height)
        k = rank[p]
        rank[p] = k + 1
        slot_ref[e] = p * CAP + k
        part = lax.div(k, 2)
        at = filled[part]
        filled[part] = at + 1
        list_ref[part * (entries // 2) + at] = e
        label = jnp.full((1, LANES), target - p * height, jnp.int32).astype(F32)
        first_ref[pl.ds(p * block + 2 * cols + k, 1), :] = label
        return carry

    lax.fori_loop(0, entries, assign, 0)
    lane = lax.broadcasted_iota(jnp.int32, (SUB, LANES), 1)

    @pl.when(ocean)
    def _():
        for copy in copies:
            copy.wait()

        def pick(e, carry):
            r = src_ref[e]
            for j in range(cols):
                melt[j, pl.ds(e, 1), :] = (
                    mask[j, pl.ds(r, 1), :].astype(F32) * fric[j, pl.ds(r, 1), :]
                ) * stress[j, pl.ds(r + HALO, 1), :]
            return carry

        lax.fori_loop(0, entries, pick, 0, unroll=2)

        def group(g, carry):
            r = pl.ds(pl.multiple_of(g * SUB, SUB), SUB)
            table = [melt[k, r, :] for k in range(cols)]
            for j in range(cols):
                s = slice(j * LANES, (j + 1) * LANES)
                index = ixbuf[r, s]
                low, high = index & (LANES - 1), index >> 7
                got = jnp.zeros((SUB, LANES), F32)
                for k in range(cols):
                    here = jnp.take_along_axis(table[k], low, axis=1, mode="promise_in_bounds")
                    got = jnp.where(high == k, here, got)
                sent[pl.ds(g * SUB * cols + j, SUB, stride=cols), :] = got * wbuf[r, s]
            return carry

        lax.fori_loop(0, entries // SUB, group, 0)

        for part, ref in enumerate((first_ref, second_ref)):
            def place(t, carry, part=part, ref=ref):
                e = list_ref[part * (entries // 2) + t]
                slot = slot_ref[e]
                p = lax.div(slot, CAP)
                row = pl.multiple_of(p * block + (slot - p * CAP - 2 * part) * cols, SUB)
                ref[pl.ds(row, cols), :] = sent[pl.ds(pl.multiple_of(e * cols, cols), cols), :]
                return carry

            lax.fori_loop(0, entries // 2, place, 0, unroll=2)

    @pl.when(ice)
    def _():
        if not zero_fill:
            for p in range(partitions):
                first_ref[p * block : p * block + 2 * cols, :] = jnp.zeros((2 * cols, LANES), F32)
        for copy in copies:
            copy.wait()
        zero = jnp.zeros((HALO, LANES), F32)
        for j in range(cols):
            for ref in (stress, ratio):
                ref[j, :HALO, :] = zero
                ref[j, HALO + height :, :] = zero

        def one_ratio(t, carry):
            r = pl.ds(pl.multiple_of(t * SUB, SUB), SUB)
            to = pl.ds(pl.multiple_of(t * SUB + HALO, SUB), SUB)
            for j in range(cols):
                ratio[j, to, :] = mask[j, r, :].astype(F32) / (2.5 + fric[j, r, :])
            return carry

        lax.fori_loop(0, height // SUB, one_ratio, 0, unroll=2)

        for i in range(rows):
            r = pl.ds(i, SUB, stride=rows)
            b = [ratio[j, r, :] for j in range(cols)]
            a = [x * stress[j, r, :] for j, x in enumerate(b)]
            for ref, regs in ((b_ref, b), (a_ref, a)):
                for j, x in enumerate(swap_bits(regs, lane, BITS)):
                    ref[i, :, j * LANES : (j + 1) * LANES] = x

        def chosen(e, carry):
            r = src_ref[e]
            for j in range(cols):
                m_rows[j, pl.ds(e, 1), :] = mask[j, pl.ds(r, 1), :]
            return carry

        lax.fori_loop(0, entries, chosen, 0, unroll=2)

        def weigh(g, carry):
            r = pl.ds(pl.multiple_of(g * SUB, SUB), SUB)
            for j in range(cols):
                s = slice(j * LANES, (j + 1) * LANES)
                gain_ref[r, s] = m_rows[j, r, :].astype(F32) * wbuf[r, s]
            return carry

        lax.fori_loop(0, entries // SUB, weigh, 0)


def prepare(section, source, destination, tie, forcing, coefficient, mask, weights, index, partitions):
    height, cells = forcing.shape
    entries = weights.shape[0]
    cols = cells // LANES
    padded = height + 2 * HALO
    sent = jax.ShapeDtypeStruct((partitions * (2 * cols + SUB), LANES), F32)
    spread = jax.ShapeDtypeStruct((padded // SUB, SUB, cells), F32)
    return pl.pallas_call(
        functools.partial(prepare_kernel, partitions * CAP != entries),
        out_shape=(
            sent, sent,
            jax.ShapeDtypeStruct((entries,), jnp.int32),
            jax.ShapeDtypeStruct((entries,), jnp.int32),
            spread, spread,
            jax.ShapeDtypeStruct((entries, cells), F32),
        ),
        in_specs=[SMEM, SMEM, SMEM, ANY] + [HBM] * 5,
        out_specs=(VMEM, VMEM, SMEM, SMEM, VMEM, VMEM, VMEM),
        scratch_shapes=[
            pltpu.VMEM((cols, padded, LANES), F32),
            pltpu.VMEM((cols, padded, LANES), F32),
            pltpu.VMEM((cols, height, LANES), F32),
            pltpu.VMEM((cols, height, LANES), jnp.int32),
            pltpu.VMEM((entries, cells), F32),
            pltpu.VMEM((entries, cells), jnp.int32),
            pltpu.VMEM((cols, entries, LANES), jnp.int32),
            pltpu.VMEM((cols, entries, LANES), F32),
            pltpu.VMEM((entries * cols, LANES), F32),
            pltpu.SMEM((partitions,), jnp.int32),
            pltpu.SMEM((2,), jnp.int32),
            pltpu.SemaphoreType.DMA((3 * cols + 2,)),
        ],
        compiler_params=params(36),
        cost_estimate=cost(10),
        name="prepare",
    )(section, source, destination, tie, forcing, coefficient, mask, weights, index)


def swap_bits(regs, lane, bits):
    regs = list(regs)
    top = len(regs).bit_length() - 1 - bits
    for b in range(bits):
        step, odd = 1 << b, (lane & (1 << b)) != 0
        apart = 1 << (top + b)
        for j in range(len(regs)):
            if j & apart:
                continue
            x, y = regs[j], regs[j + apart]
            regs[j] = jnp.where(odd, pltpu.roll(y, step, 1), x)
            regs[j + apart] = jnp.where(odd, y, pltpu.roll(x, LANES - step, 1))
    return regs


def sides(c, lane, bits):
    count = len(c)
    low = count >> bits
    step = 1 << bits
    zero = jnp.zeros((SUB, LANES), F32)
    west, east = [None] * count, [None] * count
    for j in range(count):
        if j + low < count:
            east[j] = c[j + low]
            west[j + low] = c[j]
    ahead = [pltpu.roll(c[j], LANES - step, 1) for j in range(low)]
    ahead.append(jnp.where(lane == LANES - 1, zero, pltpu.roll(c[0], LANES - step - 1, 1)))
    behind = [jnp.where(lane == 0, zero, pltpu.roll(c[count - 1], step + 1, 1))]
    behind += [pltpu.roll(c[count - low + j], step, 1) for j in range(low)]
    for j in range(low):
        east[count - low + j] = jnp.where(lane < LANES - step, ahead[j], ahead[j + 1])
        west[j] = jnp.where(lane >= step, behind[j + 1], behind[j])
    return west, east


def sweep_kernel(
    sec_ref, src_ref, a_ref, b_ref, up_ref, down_ref, gain_ref,
    vel_ref, flow_ref,
    a_halo, b_halo, v_rows, a_buf, b_buf, v_one, v_two,
):
    rows, _, cells = a_ref.shape
    cols = cells // LANES
    entries = gain_ref.shape[0]
    spans = [slice(j * LANES, (j + 1) * LANES) for j in range(cols)]

    @pl.when(sec_ref[0] == 1)
    def _():
        lane = lax.broadcasted_iota(jnp.int32, (SUB, LANES), 1)
        for k, ref in enumerate((up_ref, down_ref)):
            for t in range(HALO // SUB):
                r, q = slice(t * SUB, (t + 1) * SUB), slice(HALO + t * SUB, HALO + (t + 1) * SUB)
                b = [ref[q, s] for s in spans]
                a = [x * ref[r, s] for x, s in zip(b, spans)]
                for buf, regs in ((b_halo, b), (a_halo, a)):
                    for s, x in zip(spans, swap_bits(regs, lane, BITS)):
                        buf[k, r, s] = x
        for i in range(rows):
            for src, halo, dst in ((a_ref, a_halo, a_buf), (b_ref, b_halo, b_buf)):
                dst[i] = src[i]
                if i < HALO:
                    dst[i, 0:1, :] = halo[0, i : i + 1, :]
                if i >= rows - HALO:
                    at = i - (rows - HALO)
                    dst[i, SUB - 1 : SUB, :] = halo[1, at : at + 1, :]

        def sweep(old, store):
            north = [pltpu.roll(old[rows - 1, :, s], 1, 0) for s in spans]
            centre = [old[0, :, s] for s in spans]
            for i in range(rows):
                if i == rows - 1:
                    south = [pltpu.roll(old[0, :, s], SUB - 1, 0) for s in spans]
                else:
                    south = [old[i + 1, :, s] for s in spans]
                west, east = sides(centre, lane, BITS)
                fresh = []
                for j, s in enumerate(spans):
                    around = (north[j] + south[j]) + 0.25 * (west[j] + east[j])
                    fresh.append(a_buf[i, :, s] + b_buf[i, :, s] * around)
                store(i, fresh)
                north, centre = centre, south

        def into(buf):
            def store(i, regs):
                for x, s in zip(regs, spans):
                    buf[i, :, s] = x

            return store

        def back(i, regs):
            for j, x in enumerate(swap_bits(regs, lane, BITS)):
                vel_ref[j, pl.ds(i, SUB, stride=rows), :] = x

        def two(t, carry):
            sweep(v_two, into(v_one))
            sweep(v_one, into(v_two))
            return carry

        left = SWEEPS - 1
        sweep(a_buf, into(v_two))
        lax.fori_loop(0, (left - 2) // 2, two, 0)
        if left % 2:
            sweep(v_two, into(v_one))
            sweep(v_one, back)
        else:
            sweep(v_two, back)

        def chosen(e, carry):
            r = src_ref[e] + HALO
            for j in range(cols):
                v_rows[j, pl.ds(e, 1), :] = vel_ref[j, pl.ds(r, 1), :]
            return carry

        lax.fori_loop(0, entries, chosen, 0, unroll=2)
        zero = jnp.zeros((SUB, LANES), F32)

        def change(g, carry):
            r = pl.ds(pl.multiple_of(g * SUB, SUB), SUB)
            v = [v_rows[j, r, :] for j in range(cols)]
            ahead = [pltpu.roll(x, LANES - 1, 1) for x in v] + [zero]
            behind = [zero] + [pltpu.roll(x, 1, 1) for x in v]
            for j, s in enumerate(spans):
                east = jnp.where(lane == LANES - 1, ahead[j + 1], ahead[j])
                west = jnp.where(lane == 0, behind[j], behind[j + 1])
                flow_ref[r, s] = gain_ref[r, s] * (-0.5 * (east - west))
            return carry

        lax.fori_loop(0, entries // SUB, change, 0, unroll=2)


def all_sweeps(section, source, a, b, up, down, gain):
    rows, _, cells = a.shape
    entries = gain.shape[0]
    cols = cells // LANES
    spread = pltpu.VMEM((rows, SUB, cells), F32)
    return pl.pallas_call(
        sweep_kernel,
        out_shape=(
            jax.ShapeDtypeStruct((cols, rows * SUB, LANES), F32),
            jax.ShapeDtypeStruct((entries, cells), F32),
        ),
        in_specs=[SMEM, SMEM] + [VMEM] * 5,
        out_specs=(VMEM, VMEM),
        scratch_shapes=[
            pltpu.VMEM((2, HALO, cells), F32),
            pltpu.VMEM((2, HALO, cells), F32),
            pltpu.VMEM((cols, entries, LANES), F32),
            spread, spread, spread, spread,
        ],
        compiler_params=params(36),
        cost_estimate=cost(18),
        name="all_sweeps",
    )(section, source, a, b, up, down, gain)


def label_columns(ref, block, cols):
    partitions = ref.shape[0] // block
    return jnp.concatenate(
        [ref[pl.ds(2 * cols + k, partitions, stride=block), :] for k in range(CAP)], axis=0
    )


def row_table(pairs, j, cols):
    return jnp.concatenate(
        [
            ref[pl.ds(k * cols + j, ref.shape[0] // block, stride=block), :]
            for ref, block in pairs
            for k in range(2)
        ],
        axis=0,
    )


def values_kernel(sec_ref, handed_ref, own_ref, source_ref, gain_ref, flow_ref, out_ref):
    entries, cells = gain_ref.shape
    cols = cells // LANES
    block = 2 * cols + SUB

    @pl.when(sec_ref[0] == 1)
    def _():
        labels = label_columns(handed_ref, block, cols)[:, :entries]
        wanted = jnp.broadcast_to(source_ref[...].astype(F32), labels.shape)
        picker = jnp.transpose(jnp.where(labels == wanted, 1.0, 0.0)).astype(BF16)
        for j in range(cols):
            s = slice(j * LANES, (j + 1) * LANES)
            table = row_table(((handed_ref, block), (own_ref, block)), j, cols)
            out_ref[:, s] = flow_ref[:, s] - gain_ref[:, s] * one_hot_dot(picker, table, 3)


def thickness_values(section, handed, own, source, gain, flow):
    return pl.pallas_call(
        values_kernel,
        out_shape=jax.ShapeDtypeStruct(gain.shape, F32),
        in_specs=[SMEM] + [VMEM] * 5,
        out_specs=VMEM,
        compiler_params=params(16),
        cost_estimate=cost(1),
        name="thickness_values",
    )(section, handed, own, source, gain, flow)


HIGH = 32


def scatter_kernel(zero_fill, part, sec_ref, list_ref, slot_ref, v_ref, ix_ref, tile_ref, out_ref):
    entries, cells = v_ref.shape
    cols = cells // LANES
    count = entries // 2
    low_count = cells // HIGH
    across = LANES // low_count
    shift = low_count.bit_length() - 1
    tiled = 2 * cols + SUB
    block = 2 * cols if part else tiled
    unroll = 8 if count % 8 == 0 else 1

    @pl.when(sec_ref[0] == 1)
    def _():
        partitions = out_ref.shape[0] // block
        if zero_fill:
            out_ref[...] = jnp.zeros_like(out_ref)
        if part == 0:
            for p in range(partitions):
                at = slice(p * block + 2 * cols, (p + 1) * block)
                out_ref[at, :] = tile_ref[at, :]
        high_row = lax.broadcasted_iota(jnp.int32, (HIGH, cells), 0)
        low_row = lax.broadcasted_iota(jnp.int32, (low_count, cells), 0)

        def one(t):
            e = list_ref[part * count + t]
            slot = slot_ref[e]
            p = lax.div(slot, CAP)
            row = pl.multiple_of(p * block + (slot - p * CAP - 2 * part) * cols, SUB)
            v, index = v_ref[pl.ds(e, 1), :], ix_ref[pl.ds(e, 1), :]
            head = v.astype(BF16).astype(F32)
            rest = v - head
            upper = index >> shift
            upper = (upper & (across - 1)) * cols + (upper >> (across.bit_length() - 1))
            here = jnp.broadcast_to(upper, (HIGH, cells)) == high_row
            left = jnp.concatenate(
                [jnp.where(here, jnp.broadcast_to(x, (HIGH, cells)), 0.0) for x in (head, rest)],
                axis=0,
            ).astype(BF16)
            right = jnp.where(
                jnp.broadcast_to(index & (low_count - 1), (low_count, cells)) == low_row, 1.0, 0.0
            ).astype(BF16)
            both = lax.dot_general(
                left, right, (((1,), (1,)), ((), ())), preferred_element_type=F32
            )
            both = both[:HIGH] + both[HIGH:]
            out_ref[pl.ds(row, cols), :] = jnp.concatenate(
                [both[h * cols : (h + 1) * cols] for h in range(across)], axis=1
            )

        def some(t, carry):
            for u in range(unroll):
                one(t * unroll + u)
            return carry

        lax.fori_loop(0, count // unroll, some, 0)


def scatter_rows(part, section, lists, slot, values, index, tile, partitions):
    entries, cells = values.shape
    cols = cells // LANES
    block = 2 * cols if part else 2 * cols + SUB
    return pl.pallas_call(
        functools.partial(scatter_kernel, partitions * CAP != entries, part),
        out_shape=jax.ShapeDtypeStruct((partitions * block, LANES), F32),
        in_specs=[SMEM, SMEM, SMEM, VMEM, VMEM, ANY if part else VMEM],
        out_specs=VMEM,
        compiler_params=params(16),
        cost_estimate=cost(5),
        name="scatter_rows_%d" % part,
    )(section, lists, slot, values, index, tile)


def place_kernel(sec_ref, own_ref, handed_ref, tile_ref, m_hbm, vel_ref, out_hbm, mask, result, sems):
    height, cells = m_hbm.shape
    cols = cells // LANES
    block = 2 * cols

    @pl.when(sec_ref[0] == 0)
    def _():
        fetch = pltpu.make_async_copy(m_hbm, mask, sems.at[cols])
        fetch.start()
        labels = label_columns(tile_ref, block + SUB, cols)
        lane = lax.broadcasted_iota(jnp.int32, labels.shape, 1).astype(F32)
        picker = jnp.concatenate(
            [
                jnp.transpose(jnp.where(labels == lane + LANES * q, 1.0, 0.0))
                for q in range(height // LANES)
            ],
            axis=0,
        ).astype(BF16)
        picker = jnp.concatenate([picker] * 3, axis=1)
        fetch.wait()
        outs = []
        for j in range(cols):
            s = slice(j * LANES, (j + 1) * LANES)
            table = jnp.concatenate(
                pieces(row_table(((own_ref, block), (handed_ref, block)), j, cols), 3), axis=0
            )
            result[j] = mask[:, s].astype(F32) * jnp.dot(picker, table, preferred_element_type=F32)
            out = pltpu.make_async_copy(result.at[j], out_hbm.at[:, s], sems.at[j])
            out.start()
            outs.append(out)
        for out in outs:
            out.wait()

    @pl.when(sec_ref[0] == 1)
    def _():
        outs = [
            pltpu.make_async_copy(
                vel_ref.at[j, pl.ds(HALO, height)], out_hbm.at[:, pl.ds(j * LANES, LANES)], sems.at[j]
            )
            for j in range(cols)
        ]
        for out in outs:
            out.start()
        for out in outs:
            out.wait()


def place_rows(section, own, handed, tile, mask, velocity):
    height, cells = mask.shape
    cols = cells // LANES
    return pl.pallas_call(
        place_kernel,
        out_shape=jax.ShapeDtypeStruct((height, cells), F32),
        in_specs=[SMEM, VMEM, VMEM, VMEM, HBM, ANY],
        out_specs=HBM,
        scratch_shapes=[
            pltpu.VMEM((height, cells), jnp.int32),
            pltpu.VMEM((cols, height, LANES), F32),
            pltpu.SemaphoreType.DMA((cols + 1,)),
        ],
        compiler_params=params(16),
        cost_estimate=cost(3),
        name="place_rows",
    )(section, own, handed, tile, mask, velocity)


def per_device(forcing, coefficient, cell_mask, remap_weight, remap_index, link_source, link_target):
    partitions = lax.axis_size("dom")
    section = lax.axis_index("sect").astype(jnp.int32)
    flag = section.reshape(1)
    forcing, coefficient, mask = forcing[0], coefficient[0], cell_mask[0]
    weights, index = remap_weight[0], remap_index[0]
    source, destination = link_source.reshape(-1), link_target.reshape(-1)
    cells = forcing.shape[1]
    cols = cells // LANES

    both = ("sect", "dom")
    to_ice = [(i, partitions + i) for i in range(partitions)]
    to_ocean = [(partitions + i, i) for i in range(partitions)]
    onward = [(partitions + i, partitions + i + 1) for i in range(partitions - 1)]

    def exchange(x):
        return lax.all_to_all(x, "dom", 0, 0, tiled=True).reshape(-1, LANES)

    last, start = halo_rows(flag, forcing, coefficient, mask)
    up = lax.ppermute(last, both, onward)
    down = lax.ppermute(start, both, [(j, i) for i, j in onward])
    first, second, slot, lists, a, b, gain = prepare(
        flag, source, destination, last, forcing, coefficient, mask, weights, index, partitions
    )
    second = lax.ppermute(second, both, to_ice)
    arrived = exchange((first + second).reshape(partitions, -1, LANES))
    velocity, flow = all_sweeps(flag, source, a, b, up, down, gain)
    handed = lax.ppermute(arrived, both, to_ice)
    values = thickness_values(flag, handed, arrived, link_source, gain, flow)
    first = scatter_rows(0, flag, lists, slot, values, index, arrived, partitions)
    tile = lax.ppermute(first, both, to_ocean)
    second = scatter_rows(1, flag, lists, slot, values, index, first, partitions)
    mine = tile.reshape(partitions, -1, LANES)[:, : 2 * cols]
    arrived = exchange(jnp.where(section == 0, mine, second.reshape(partitions, -1, LANES)))
    handed = lax.ppermute(arrived, both, to_ocean)
    return place_rows(flag, arrived, handed, tile, mask, velocity)[None]


def solution(mesh):
    in_specs = (P("sect", "dom", None),) * 5 + (P("sect", "dom"),) * 2
    return jax.shard_map(
        per_device, mesh=mesh, in_specs=in_specs, out_specs=P("sect", "dom", None), check_vma=False
    )
```

```python
import functools

import jax
import jax.numpy as jnp
from jax import lax
from jax.experimental import pallas as pl
from jax.experimental.pallas import tpu as pltpu
from jax.sharding import PartitionSpec as P

CAP = 4
SWEEPS = 20
LANES = 128
SUB = 8
HALO = 24
BITS = 2

F32 = jnp.float32
BF16 = jnp.bfloat16
ANY = pl.BlockSpec(memory_space=pl.ANY)
HBM = pl.BlockSpec(memory_space=pltpu.HBM)
VMEM = pl.BlockSpec(memory_space=pltpu.VMEM)
SMEM = pl.BlockSpec(memory_space=pltpu.SMEM)


def params(mib):
    return pltpu.CompilerParams(vmem_limit_bytes=mib * 2**20)


def in_hbm(*arrays):
    return [pltpu.with_memory_space_constraint(x, pltpu.HBM) for x in arrays]


def cost(microseconds):
    return pl.CostEstimate(flops=0, bytes_accessed=int(microseconds * 3.0e6), transcendentals=0)


def pieces(x, count):
    out = []
    for _ in range(count - 1):
        head = x.astype(BF16)
        out.append(head)
        x = x - head.astype(F32)
    out.append(x.astype(BF16))
    return out


def one_hot_dot(picker, table, count):
    total = None
    for piece in pieces(table, count):
        part = jnp.dot(picker, piece, preferred_element_type=F32)
        total = part if total is None else total + part
    return total


def swap_matrix():
    wide, low = LANES << BITS, (1 << BITS) - 1
    here = lax.broadcasted_iota(jnp.int32, (wide, wide), 0)
    there = lax.broadcasted_iota(jnp.int32, (wide, wide), 1)
    lane, group = here & (LANES - 1), here >> 7
    goal = (lane & low) * LANES + (lane - (lane & low)) + group
    return jnp.where(goal == there, 1.0, 0.0).astype(BF16)


def swap_bits(blocks, matrix):
    count, rows = len(blocks), blocks[0].shape[0]
    low = count >> BITS
    stacked = [[] for _ in range(3)]
    for j in range(low):
        x = jnp.concatenate(blocks[j::low], axis=1)
        for k in range(2):
            head = x.astype(BF16).astype(F32)
            stacked[k].append(head)
            x = x - head
        stacked[2].append(x)
    left = jnp.concatenate(sum(stacked, []), axis=0).astype(BF16)
    out = jnp.dot(left, matrix, preferred_element_type=F32)
    size = low * rows
    out = out[:size] + out[size : 2 * size] + out[2 * size :]
    return [
        out[j * rows : (j + 1) * rows, o * LANES : (o + 1) * LANES]
        for o in range(1 << BITS)
        for j in range(low)
    ]


def sides(c, lane, bits):
    count = len(c)
    low = count >> bits
    step = 1 << bits
    zero = jnp.zeros((SUB, LANES), F32)
    west, east = [None] * count, [None] * count
    for j in range(count):
        if j + low < count:
            east[j] = c[j + low]
            west[j + low] = c[j]
    ahead = [pltpu.roll(c[j], LANES - step, 1) for j in range(low)]
    ahead.append(jnp.where(lane == LANES - 1, zero, pltpu.roll(c[0], LANES - step - 1, 1)))
    behind = [jnp.where(lane == 0, zero, pltpu.roll(c[count - 1], step + 1, 1))]
    behind += [pltpu.roll(c[count - low + j], step, 1) for j in range(low)]
    for j in range(low):
        east[count - low + j] = jnp.where(lane < LANES - step, ahead[j], ahead[j + 1])
        west[j] = jnp.where(lane >= step, behind[j + 1], behind[j])
    return west, east


DEEP = HALO // SUB


def halo_kernel(sec_ref, f_hbm, c_hbm, m_hbm, last_ref, first_ref, stress, fric, mask, nat, sems):
    height, cells = f_hbm.shape
    cols = cells // LANES
    spans = [slice(j * LANES, (j + 1) * LANES) for j in range(cols)]

    @pl.when(sec_ref[0] == 1)
    def _():
        copies = []
        for k, start in enumerate((height - HALO, 0)):
            for src, dst in ((f_hbm, stress), (c_hbm, fric), (m_hbm, mask)):
                copy = pltpu.make_async_copy(src.at[pl.ds(start, HALO)], dst.at[k], sems.at[len(copies)])
                copy.start()
                copies.append(copy)
        matrix = swap_matrix()
        for copy in copies:
            copy.wait()
        for k, ref in enumerate((last_ref, first_ref)):
            b = [mask[k, :, s].astype(F32) / (2.5 + fric[k, :, s]) for s in spans]
            a = [x * stress[k, :, s] for x, s in zip(b, spans)]
            both = [jnp.concatenate([x, y], axis=0) for x, y in zip(a, b)]
            for j, x in enumerate(swap_bits(both, matrix)):
                nat[k, j] = x
            for q in range(2):
                for i in range(DEEP):
                    for j, s in enumerate(spans):
                        ref[q * DEEP + i, :, s] = nat[k, j, pl.ds(q * HALO + i, SUB, stride=DEEP), :]


def halo_rows(section, forcing, coefficient, mask):
    cells = forcing.shape[1]
    cols = cells // LANES
    out = jax.ShapeDtypeStruct((2 * DEEP, SUB, cells), F32)
    return pl.pallas_call(
        halo_kernel,
        out_shape=(out, out),
        in_specs=[SMEM, HBM, HBM, HBM],
        out_specs=(VMEM, VMEM),
        scratch_shapes=[
            pltpu.VMEM((2, HALO, cells), F32),
            pltpu.VMEM((2, HALO, cells), F32),
            pltpu.VMEM((2, HALO, cells), jnp.int32),
            pltpu.VMEM((2, cols, 2 * HALO, LANES), F32),
            pltpu.SemaphoreType.DMA((6,)),
        ],
        compiler_params=params(16),
        cost_estimate=cost(2),
        name="halo_rows",
    )(section, *in_hbm(forcing, coefficient, mask))


def melt_kernel(
    zero_fill, sec_ref, src_ref, tgt_ref, tie_ref, f_hbm, c_hbm, m_hbm, w_hbm, ix_hbm,
    outbox, stress, fric, mask, wbuf, ixbuf, sent, slots, rank, sems,
):
    del tie_ref
    height = f_hbm.shape[0]
    entries, cells = w_hbm.shape
    cols = cells // LANES
    block = CAP * cols + SUB
    partitions = rank.shape[0]
    spans = [slice(j * LANES, (j + 1) * LANES) for j in range(cols)]
    grids = ((f_hbm, stress), (c_hbm, fric), (m_hbm, mask))

    @pl.when(sec_ref[0] == 0)
    def _():
        for q, (src, dst) in enumerate(grids):
            def one(e, carry, q=q, src=src, dst=dst):
                pltpu.make_async_copy(
                    src.at[pl.ds(src_ref[e], 1)], dst.at[pl.ds(e, 1)], sems.at[q]
                ).start()
                return carry

            lax.fori_loop(0, entries, one, 0, unroll=4)
        whole = [
            pltpu.make_async_copy(src, dst, sems.at[3 + k])
            for k, (src, dst) in enumerate(((ix_hbm, ixbuf), (w_hbm, wbuf)))
        ]
        for copy in whole:
            copy.start()
        for p in range(partitions):
            rank[p] = 0
            at = p * block + CAP * cols
            outbox[at : at + SUB, :] = jnp.full((SUB, LANES), -1.0, F32)
            if zero_fill:
                outbox[p * block : at, :] = jnp.zeros((CAP * cols, LANES), F32)

        def assign(e, carry):
            target = tgt_ref[e]
            p = lax.div(target, height)
            k = rank[p]
            rank[p] = k + 1
            row = p * block
            slots[e] = row + k * cols
            label = jnp.full((1, LANES), target - p * height, jnp.int32).astype(F32)
            outbox[pl.ds(row + CAP * cols + k, 1), :] = label
            return carry

        lax.fori_loop(0, entries, assign, 0)
        for q, (src, dst) in enumerate(grids):
            at = pl.ds(0, entries)
            pltpu.make_async_copy(src.at[at], dst.at[at], sems.at[q]).wait()
        for copy in whole:
            copy.wait()

        def group(g, carry):
            r = pl.ds(pl.multiple_of(g * SUB, SUB), SUB)
            table = [mask[r, s].astype(F32) * fric[r, s] * stress[r, s] for s in spans]
            for j, s in enumerate(spans):
                index = ixbuf[r, s]
                low, high = index & (LANES - 1), index >> 7
                got = [
                    jnp.take_along_axis(x, low, axis=1, mode="promise_in_bounds") for x in table
                ]
                bit = 1
                while len(got) > 1:
                    odd = (high & bit) != 0
                    got = [jnp.where(odd, got[t + 1], got[t]) for t in range(0, len(got), 2)]
                    bit *= 2
                sent[pl.ds(g * SUB * cols + j, SUB, stride=cols), :] = got[0] * wbuf[r, s]
            return carry

        lax.fori_loop(0, entries // SUB, group, 0)

        def place(e, carry):
            row = pl.multiple_of(slots[e], SUB)
            outbox[pl.ds(row, cols), :] = sent[pl.ds(pl.multiple_of(e * cols, cols), cols), :]
            return carry

        lax.fori_loop(0, entries, place, 0, unroll=4)

    @pl.when(sec_ref[0] == 1)
    def _():
        outbox[...] = jnp.zeros_like(outbox)


def melt_rows(section, source, destination, before, forcing, coefficient, mask, weights, index, partitions):
    entries, cells = weights.shape
    cols = cells // LANES
    return pl.pallas_call(
        functools.partial(melt_kernel, partitions * CAP != entries),
        out_shape=jax.ShapeDtypeStruct((partitions * (CAP * cols + SUB), LANES), F32),
        in_specs=[SMEM, SMEM, SMEM, ANY] + [HBM] * 5,
        out_specs=VMEM,
        scratch_shapes=[
            pltpu.VMEM((entries, cells), F32),
            pltpu.VMEM((entries, cells), F32),
            pltpu.VMEM((entries, cells), jnp.int32),
            pltpu.VMEM((entries, cells), F32),
            pltpu.VMEM((entries, cells), jnp.int32),
            pltpu.VMEM((entries * cols, LANES), F32),
            pltpu.SMEM((entries,), jnp.int32),
            pltpu.SMEM((partitions,), jnp.int32),
            pltpu.SemaphoreType.DMA((5,)),
        ],
        compiler_params=params(16),
        cost_estimate=cost(8),
        name="melt_rows",
    )(section, source, destination, before, *in_hbm(forcing, coefficient, mask, weights, index))


def tie_kernel(*refs):
    del refs


def tie(value, *before):
    return pl.pallas_call(
        tie_kernel,
        out_shape=jax.ShapeDtypeStruct(value.shape, value.dtype),
        in_specs=[ANY] * (1 + len(before)),
        out_specs=ANY,
        input_output_aliases={0: 0},
        compiler_params=params(1),
        cost_estimate=cost(0.1),
        name="tie",
    )(value, *before)


def sweep_tools(a_ref, b_ref, up_ref, down_ref):
    own, _, cells = a_ref.shape
    cols = cells // LANES
    spans = [slice(j * LANES, (j + 1) * LANES) for j in range(cols)]
    lane = lax.broadcasted_iota(jnp.int32, (SUB, LANES), 1)
    sub = lax.broadcasted_iota(jnp.int32, (SUB, LANES), 0)
    groups = ((0, DEEP), (DEEP, own), (DEEP + own, DEEP))

    def known(which, i, s):
        if i < DEEP:
            return up_ref[which * DEEP + i, :, s]
        if i < DEEP + own:
            return (a_ref, b_ref)[which][i - DEEP, :, s]
        return down_ref[which * DEEP + i - DEEP - own, :, s]

    def sweep(old, store):
        def row(i):
            return [old(i, s) for s in spans]

        for k, (start, count) in enumerate(groups):
            north = [pltpu.roll(x, 1, 0) for x in row(start + count - 1)]
            if k > 0:
                north = [jnp.where(sub == 0, pltpu.roll(x, 1, 0), y) for x, y in zip(row(start - 1), north)]
            centre = row(start)
            for i in range(start, start + count):
                if i < start + count - 1:
                    south = row(i + 1)
                else:
                    south = [pltpu.roll(x, SUB - 1, 0) for x in row(start)]
                    if k < 2:
                        south = [
                            jnp.where(sub == SUB - 1, pltpu.roll(x, SUB - 1, 0), y)
                            for x, y in zip(row(i + 1), south)
                        ]
                west, east = sides(centre, lane, BITS)
                fresh = []
                for j, s in enumerate(spans):
                    around = (north[j] + south[j]) + 0.25 * (west[j] + east[j])
                    fresh.append(known(0, i, s) + known(1, i, s) * around)
                store(i, fresh)
                north, centre = centre, south

    def of(buf):
        return lambda i, s: buf[i, :, s]

    def into(buf):
        def store(i, regs):
            for x, s in zip(regs, spans):
                buf[i, :, s] = x

        return store

    return spans, lane, sweep, lambda i, s: known(0, i, s), of, into


def ice_kernel(
    sec_ref, src_ref, tgt_ref, up_ref, down_ref, f_hbm, c_hbm, m_hbm, w_hbm,
    vel_hbm, flow_ref, gain_ref, tile_ref, slot_ref, list_ref,
    stress, fric, mask, wbuf, a_nat, b_nat, a_ref, b_ref, v_one, v_two, m_rows, v_rows, rank, filled, sems,
):
    height, cells = f_hbm.shape
    entries = w_hbm.shape[0]
    cols = cells // LANES
    partitions = rank.shape[0]
    rows = height // SUB
    chunks = 4
    size = height // chunks
    grids = ((f_hbm, stress), (c_hbm, fric), (m_hbm, mask))

    def part_copy(q, k):
        at = pl.ds(k * size, size)
        return pltpu.make_async_copy(grids[q][0].at[at], grids[q][1].at[at], sems.at[q * chunks + k])

    @pl.when(sec_ref[0] == 1)
    def _():
        for k in range(chunks):
            for q in range(3):
                part_copy(q, k).start()
        weight_copy = pltpu.make_async_copy(w_hbm, wbuf, sems.at[3 * chunks])
        weight_copy.start()
        tile_ref[...] = jnp.full(tile_ref.shape, -1.0, F32)
        for p in range(partitions):
            rank[p] = 0
        filled[0] = 0
        filled[1] = 0

        def assign(e, carry):
            target = tgt_ref[e]
            p = lax.div(target, height)
            k = rank[p]
            rank[p] = k + 1
            slot_ref[e] = p * CAP + k
            part = lax.div(k, 2)
            at = filled[part]
            filled[part] = at + 1
            list_ref[part * (entries // 2) + at] = e
            label = jnp.full((1, LANES), target - p * height, jnp.int32).astype(F32)
            tile_ref[pl.ds(p * SUB + k, 1), :] = label
            return carry

        lax.fori_loop(0, entries, assign, 0)
        spans, lane, sweep, start, of, into = sweep_tools(a_ref, b_ref, up_ref, down_ref)
        matrix = swap_matrix()
        for k in range(chunks):
            for q in range(3):
                part_copy(q, k).wait()
            r = slice(k * size, (k + 1) * size)
            b = [mask[r, s].astype(F32) / (2.5 + fric[r, s]) for s in spans]
            a = [x * stress[r, s] for x, s in zip(b, spans)]
            for nat, blocks in ((b_nat, b), (a_nat, a)):
                for j, x in enumerate(swap_bits(blocks, matrix)):
                    for t in range(k * (size // SUB), (k + 1) * (size // SUB)):
                        to = t * SUB
                        nat[j, to : to + SUB, :] = x[t * SUB - k * size : (t + 1) * SUB - k * size]
        for i in range(rows):
            r = pl.ds(i, SUB, stride=rows)
            for ref, nat in ((b_ref, b_nat), (a_ref, a_nat)):
                for j, s in enumerate(spans):
                    ref[i, :, s] = nat[j, r, :]

        def two(t, carry):
            sweep(of(v_one), into(v_two))
            sweep(of(v_two), into(v_one))
            return carry

        left = SWEEPS - 2
        sweep(start, into(v_one))
        lax.fori_loop(0, left // 2, two, 0)
        last = v_one
        if left % 2:
            sweep(of(v_one), into(v_two))
            last = v_two
        velocity = a_nat
        some = 8 if rows % 8 == 0 else rows
        for t in range(rows // some):
            at = slice(DEEP + t * some, DEEP + (t + 1) * some)
            blocks = [last[at, :, s].reshape(some * SUB, LANES) for s in spans]
            for j, x in enumerate(swap_bits(blocks, matrix)):
                for i in range(some):
                    velocity[j, pl.ds(t * some + i, SUB, stride=rows), :] = x[i * SUB : (i + 1) * SUB]
        outs = [
            pltpu.make_async_copy(velocity.at[j], vel_hbm.at[:, pl.ds(j * LANES, LANES)], sems.at[j])
            for j in range(cols)
        ]
        for out in outs:
            out.start()
        weight_copy.wait()

        def chosen(e, carry):
            at, r = pl.ds(e, 1), pl.ds(src_ref[e], 1)
            row = mask[r, :]
            for j, s in enumerate(spans):
                m_rows[j, at, :] = row[:, s]
                v_rows[j, at, :] = velocity[j, r, :]
            return carry

        lax.fori_loop(0, entries, chosen, 0, unroll=4)
        zero = jnp.zeros((SUB, LANES), F32)

        for g in range(entries // SUB):
            r = slice(g * SUB, (g + 1) * SUB)
            v = [v_rows[j, r, :] for j in range(cols)]
            ahead = [pltpu.roll(x, LANES - 1, 1) for x in v] + [zero]
            behind = [zero] + [pltpu.roll(x, 1, 1) for x in v]
            for j, s in enumerate(spans):
                east = jnp.where(lane == LANES - 1, ahead[j + 1], ahead[j])
                west = jnp.where(lane == 0, behind[j], behind[j + 1])
                gain = m_rows[j, r, :].astype(F32) * wbuf[r, s]
                gain_ref[r, s] = gain
                flow_ref[r, s] = gain * (-0.5 * (east - west))
        for out in outs:
            out.wait()


def ice_sweeps(section, source, destination, up, down, forcing, coefficient, mask, weights, partitions):
    height, cells = forcing.shape
    entries = weights.shape[0]
    cols = cells // LANES
    rows = height // SUB
    chosen = jax.ShapeDtypeStruct((entries, cells), F32)
    numbers = jax.ShapeDtypeStruct((entries,), jnp.int32)
    own = pltpu.VMEM((rows, SUB, cells), F32)
    spread = pltpu.VMEM((rows + 2 * DEEP, SUB, cells), F32)
    return pl.pallas_call(
        ice_kernel,
        out_shape=(
            jax.ShapeDtypeStruct((height, cells), F32), chosen, chosen,
            jax.ShapeDtypeStruct((partitions * SUB, LANES), F32), numbers, numbers,
        ),
        in_specs=[SMEM] * 3 + [VMEM] * 2 + [HBM] * 4,
        out_specs=(HBM, VMEM, VMEM, VMEM, SMEM, SMEM),
        scratch_shapes=[
            pltpu.VMEM((height, cells), F32),
            pltpu.VMEM((height, cells), F32),
            pltpu.VMEM((height, cells), jnp.int32),
            pltpu.VMEM((entries, cells), F32),
            pltpu.VMEM((cols, height, LANES), F32),
            pltpu.VMEM((cols, height, LANES), F32),
            own, own, spread, spread,
            pltpu.VMEM((cols, entries, LANES), jnp.int32),
            pltpu.VMEM((cols, entries, LANES), F32),
            pltpu.SMEM((partitions,), jnp.int32),
            pltpu.SMEM((2,), jnp.int32),
            pltpu.SemaphoreType.DMA((max(3 * 4 + 1, cols),)),
        ],
        compiler_params=params(48),
        cost_estimate=cost(24),
        name="ice_sweeps",
    )(section, source, destination, up, down, *in_hbm(forcing, coefficient, mask, weights))


def label_columns(ref, block):
    partitions = ref.shape[0] // block
    return jnp.concatenate(
        [ref[pl.ds(block - SUB + k, partitions, stride=block), :] for k in range(CAP)], axis=0
    )


def row_table(refs, block, ranks, j, cols):
    return jnp.concatenate(
        [
            ref[pl.ds(k * cols + j, ref.shape[0] // block, stride=block), :]
            for ref in refs
            for k in range(ranks)
        ],
        axis=0,
    )


def values_kernel(sec_ref, handed_ref, source_ref, gain_ref, flow_ref, out_ref):
    entries, cells = gain_ref.shape
    cols = cells // LANES
    block = CAP * cols + SUB

    @pl.when(sec_ref[0] == 1)
    def _():
        labels = label_columns(handed_ref, block)[:, :entries]
        wanted = jnp.broadcast_to(source_ref[...].astype(F32), labels.shape)
        picker = jnp.transpose(jnp.where(labels == wanted, 1.0, 0.0)).astype(BF16)
        for j in range(cols):
            s = slice(j * LANES, (j + 1) * LANES)
            table = row_table((handed_ref,), block, CAP, j, cols)
            out_ref[:, s] = flow_ref[:, s] - gain_ref[:, s] * one_hot_dot(picker, table, 3)


def thickness_values(section, handed, source, gain, flow):
    return pl.pallas_call(
        values_kernel,
        out_shape=jax.ShapeDtypeStruct(gain.shape, F32),
        in_specs=[SMEM] + [VMEM] * 4,
        out_specs=VMEM,
        compiler_params=params(16),
        cost_estimate=cost(1),
        name="thickness_values",
    )(section, handed, source, gain, flow)


HIGH = 32


def scatter_kernel(zero_fill, part, sec_ref, list_ref, slot_ref, v_ref, ix_ref, tile_ref, out_ref):
    entries, cells = v_ref.shape
    cols = cells // LANES
    count = entries // 2
    low_count = cells // HIGH
    across = LANES // low_count
    shift = low_count.bit_length() - 1
    block = 2 * cols + SUB
    unroll = 8 if count % 8 == 0 else 1

    @pl.when(sec_ref[0] == 1)
    def _():
        partitions = out_ref.shape[0] // block
        if zero_fill:
            out_ref[...] = jnp.zeros_like(out_ref)
        for p in range(partitions):
            out_ref[p * block + 2 * cols : (p + 1) * block, :] = tile_ref[p * SUB : (p + 1) * SUB, :]
        high_row = lax.broadcasted_iota(jnp.int32, (HIGH, cells), 0)
        low_row = lax.broadcasted_iota(jnp.int32, (low_count, cells), 0)

        def one(t):
            e = list_ref[part * count + t]
            slot = slot_ref[e]
            p = lax.div(slot, CAP)
            row = pl.multiple_of(p * block + (slot - p * CAP - 2 * part) * cols, SUB)
            v, index = v_ref[pl.ds(e, 1), :], ix_ref[pl.ds(e, 1), :]
            head = v.astype(BF16).astype(F32)
            rest = v - head
            upper = index >> shift
            upper = (upper & (across - 1)) * cols + (upper >> (across.bit_length() - 1))
            here = jnp.broadcast_to(upper, (HIGH, cells)) == high_row
            left = jnp.concatenate(
                [jnp.where(here, jnp.broadcast_to(x, (HIGH, cells)), 0.0) for x in (head, rest)],
                axis=0,
            ).astype(BF16)
            right = jnp.where(
                jnp.broadcast_to(index & (low_count - 1), (low_count, cells)) == low_row, 1.0, 0.0
            ).astype(BF16)
            both = lax.dot_general(
                left, right, (((1,), (1,)), ((), ())), preferred_element_type=F32
            )
            both = both[:HIGH] + both[HIGH:]
            out_ref[pl.ds(row, cols), :] = jnp.concatenate(
                [both[h * cols : (h + 1) * cols] for h in range(across)], axis=1
            )

        def some(t, carry):
            for u in range(unroll):
                one(t * unroll + u)
            return carry

        lax.fori_loop(0, count // unroll, some, 0)


def scatter_rows(part, section, lists, slot, values, index, tile, partitions):
    entries, cells = values.shape
    cols = cells // LANES
    block = 2 * cols + SUB
    return pl.pallas_call(
        functools.partial(scatter_kernel, partitions * CAP != entries, part),
        out_shape=jax.ShapeDtypeStruct((partitions * block, LANES), F32),
        in_specs=[SMEM, SMEM, SMEM, VMEM, VMEM, VMEM],
        out_specs=VMEM,
        compiler_params=params(16),
        cost_estimate=cost(5),
        name="scatter_rows_%d" % part,
    )(section, lists, slot, values, index, tile)


def place_kernel(sec_ref, own_ref, handed_ref, m_hbm, vel_hbm, out_hbm, mask, result, sems):
    del vel_hbm
    height, cells = m_hbm.shape
    cols = cells // LANES
    block = 2 * cols + SUB

    @pl.when(sec_ref[0] == 0)
    def _():
        fetch = pltpu.make_async_copy(m_hbm, mask, sems.at[cols])
        fetch.start()
        labels = label_columns(own_ref, block)
        lane = lax.broadcasted_iota(jnp.int32, labels.shape, 1).astype(F32)
        picker = jnp.concatenate(
            [
                jnp.transpose(jnp.where(labels == lane + LANES * q, 1.0, 0.0))
                for q in range(height // LANES)
            ],
            axis=0,
        ).astype(BF16)
        picker = jnp.concatenate([picker] * 3, axis=1)
        fetch.wait()
        outs = []
        for j in range(cols):
            s = slice(j * LANES, (j + 1) * LANES)
            table = jnp.concatenate(
                pieces(row_table((own_ref, handed_ref), block, 2, j, cols), 3), axis=0
            )
            result[j] = mask[:, s].astype(F32) * jnp.dot(picker, table, preferred_element_type=F32)
            out = pltpu.make_async_copy(result.at[j], out_hbm.at[:, s], sems.at[j])
            out.start()
            outs.append(out)
        for out in outs:
            out.wait()


def place_rows(section, own, handed, mask, velocity):
    height, cells = mask.shape
    cols = cells // LANES
    return pl.pallas_call(
        place_kernel,
        out_shape=jax.ShapeDtypeStruct((height, cells), F32),
        in_specs=[SMEM, VMEM, VMEM, HBM, HBM],
        out_specs=HBM,
        input_output_aliases={4: 0},
        scratch_shapes=[
            pltpu.VMEM((height, cells), jnp.int32),
            pltpu.VMEM((cols, height, LANES), F32),
            pltpu.SemaphoreType.DMA((cols + 1,)),
        ],
        compiler_params=params(16),
        cost_estimate=cost(3),
        name="place_rows",
    )(section, own, handed, *in_hbm(mask, velocity))


def per_device(forcing, coefficient, cell_mask, remap_weight, remap_index, link_source, link_target):
    partitions = lax.axis_size("dom")
    section = lax.axis_index("sect").astype(jnp.int32)
    flag = section.reshape(1)
    forcing, coefficient, mask = forcing[0], coefficient[0], cell_mask[0]
    weights, index = remap_weight[0], remap_index[0]
    source, destination = link_source.reshape(-1), link_target.reshape(-1)
    cells = forcing.shape[1]
    cols = cells // LANES

    both = ("sect", "dom")
    to_ice = [(i, partitions + i) for i in range(partitions)]
    to_ocean = [(partitions + i, i) for i in range(partitions)]
    onward = [(partitions + i, partitions + i + 1) for i in range(partitions - 1)]

    def exchange(x):
        return lax.all_to_all(x, "dom", 0, 0, tiled=True).reshape(-1, LANES)

    last, start = halo_rows(flag, forcing, coefficient, mask)
    up = lax.ppermute(last, both, onward)
    down = lax.ppermute(start, both, [(j, i) for i, j in onward])
    outbox = melt_rows(
        flag, source, destination, last, forcing, coefficient, mask, weights, index, partitions
    )
    arrived = exchange(tie(outbox, up, down).reshape(partitions, -1, LANES))
    velocity, flow, gain, tile, slot, lists = ice_sweeps(
        flag, source, destination, up, down, forcing, coefficient, mask, weights, partitions
    )
    handed = lax.ppermute(tie(arrived, flow), both, to_ice)
    values = thickness_values(flag, handed, link_source, gain, flow)
    first = scatter_rows(0, flag, lists, slot, values, index, tile, partitions)
    second = scatter_rows(1, flag, lists, slot, values, index, tile, partitions)
    first = lax.ppermute(first, both, to_ocean)
    arrived = exchange(jnp.where(section == 0, first, second).reshape(partitions, -1, LANES))
    handed = lax.ppermute(arrived, both, to_ocean)
    return place_rows(flag, arrived, handed, mask, velocity)[None]


def solution(mesh):
    in_specs = (P("sect", "dom", None),) * 5 + (P("sect", "dom"),) * 2
    return jax.shard_map(
        per_device, mesh=mesh, in_specs=in_specs, out_specs=P("sect", "dom", None), check_vma=False
    )
```

```python
import functools

import jax
import jax.numpy as jnp
from jax import lax
from jax.experimental import pallas as pl
from jax.experimental.pallas import tpu as pltpu
from jax.sharding import PartitionSpec as P

CAP = 4
SWEEPS = 20
LANES = 128
SUB = 8
HALO = 24
BITS = 2

F32 = jnp.float32
BF16 = jnp.bfloat16
ANY = pl.BlockSpec(memory_space=pl.ANY)
HBM = pl.BlockSpec(memory_space=pltpu.HBM)
VMEM = pl.BlockSpec(memory_space=pltpu.VMEM)
SMEM = pl.BlockSpec(memory_space=pltpu.SMEM)


def params(mib):
    return pltpu.CompilerParams(vmem_limit_bytes=mib * 2**20)


def in_hbm(*arrays):
    return [pltpu.with_memory_space_constraint(x, pltpu.HBM) for x in arrays]


def cost(microseconds):
    return pl.CostEstimate(flops=0, bytes_accessed=int(microseconds * 3.0e6), transcendentals=0)


def pieces(x, count):
    out = []
    for _ in range(count - 1):
        head = x.astype(BF16)
        out.append(head)
        x = x - head.astype(F32)
    out.append(x.astype(BF16))
    return out


def one_hot_dot(picker, table, count):
    total = None
    for piece in pieces(table, count):
        part = jnp.dot(picker, piece, preferred_element_type=F32)
        total = part if total is None else total + part
    return total


def swap_matrix():
    wide, low = LANES << BITS, (1 << BITS) - 1
    here = lax.broadcasted_iota(jnp.int32, (wide, wide), 0)
    there = lax.broadcasted_iota(jnp.int32, (wide, wide), 1)
    lane, group = here & (LANES - 1), here >> 7
    goal = (lane & low) * LANES + (lane - (lane & low)) + group
    return jnp.where(goal == there, 1.0, 0.0).astype(BF16)


def swap_bits(blocks, matrix):
    count, rows = len(blocks), blocks[0].shape[0]
    low = count >> BITS
    stacked = [[] for _ in range(3)]
    for j in range(low):
        x = jnp.concatenate(blocks[j::low], axis=1)
        for k in range(2):
            head = x.astype(BF16).astype(F32)
            stacked[k].append(head)
            x = x - head
        stacked[2].append(x)
    left = jnp.concatenate(sum(stacked, []), axis=0).astype(BF16)
    out = jnp.dot(left, matrix, preferred_element_type=F32)
    size = low * rows
    out = out[:size] + out[size : 2 * size] + out[2 * size :]
    return [
        out[j * rows : (j + 1) * rows, o * LANES : (o + 1) * LANES]
        for o in range(1 << BITS)
        for j in range(low)
    ]


def sides(c, lane, bits):
    count = len(c)
    low = count >> bits
    step = 1 << bits
    zero = jnp.zeros((SUB, LANES), F32)
    west, east = [None] * count, [None] * count
    for j in range(count):
        if j + low < count:
            east[j] = c[j + low]
            west[j + low] = c[j]
    ahead = [pltpu.roll(c[j], LANES - step, 1) for j in range(low)]
    ahead.append(jnp.where(lane == LANES - 1, zero, pltpu.roll(c[0], LANES - step - 1, 1)))
    behind = [jnp.where(lane == 0, zero, pltpu.roll(c[count - 1], step + 1, 1))]
    behind += [pltpu.roll(c[count - low + j], step, 1) for j in range(low)]
    for j in range(low):
        east[count - low + j] = jnp.where(lane < LANES - step, ahead[j], ahead[j + 1])
        west[j] = jnp.where(lane >= step, behind[j + 1], behind[j])
    return west, east


DEEP = HALO // SUB


def halo_kernel(sec_ref, f_hbm, c_hbm, m_hbm, last_ref, first_ref, stress, fric, mask, nat, sems):
    height, cells = f_hbm.shape
    cols = cells // LANES
    spans = [slice(j * LANES, (j + 1) * LANES) for j in range(cols)]

    @pl.when(sec_ref[0] == 1)
    def _():
        copies = []
        for k, start in enumerate((height - HALO, 0)):
            for src, dst in ((f_hbm, stress), (c_hbm, fric), (m_hbm, mask)):
                copy = pltpu.make_async_copy(src.at[pl.ds(start, HALO)], dst.at[k], sems.at[len(copies)])
                copy.start()
                copies.append(copy)
        matrix = swap_matrix()
        for copy in copies:
            copy.wait()
        for k, ref in enumerate((last_ref, first_ref)):
            b = [mask[k, :, s].astype(F32) / (2.5 + fric[k, :, s]) for s in spans]
            a = [x * stress[k, :, s] for x, s in zip(b, spans)]
            both = [jnp.concatenate([x, y], axis=0) for x, y in zip(a, b)]
            for j, x in enumerate(swap_bits(both, matrix)):
                nat[k, j] = x
            for q in range(2):
                for i in range(DEEP):
                    for j, s in enumerate(spans):
                        ref[q * DEEP + i, :, s] = nat[k, j, pl.ds(q * HALO + i, SUB, stride=DEEP), :]


def halo_rows(section, forcing, coefficient, mask):
    cells = forcing.shape[1]
    cols = cells // LANES
    out = jax.ShapeDtypeStruct((2 * DEEP, SUB, cells), F32)
    return pl.pallas_call(
        halo_kernel,
        out_shape=(out, out),
        in_specs=[SMEM, HBM, HBM, HBM],
        out_specs=(VMEM, VMEM),
        scratch_shapes=[
            pltpu.VMEM((2, HALO, cells), F32),
            pltpu.VMEM((2, HALO, cells), F32),
            pltpu.VMEM((2, HALO, cells), jnp.int32),
            pltpu.VMEM((2, cols, 2 * HALO, LANES), F32),
            pltpu.SemaphoreType.DMA((6,)),
        ],
        compiler_params=params(16),
        cost_estimate=cost(2),
        name="halo_rows",
    )(section, *in_hbm(forcing, coefficient, mask))


def melt_kernel(
    zero_fill, sec_ref, src_ref, tgt_ref, tie_ref, f_hbm, c_hbm, m_hbm, w_hbm, ix_hbm,
    outbox, stress, fric, mask, wbuf, ixbuf, sent, slots, rank, sems,
):
    del tie_ref
    height = f_hbm.shape[0]
    entries, cells = w_hbm.shape
    cols = cells // LANES
    block = CAP * cols + SUB
    partitions = rank.shape[0]
    spans = [slice(j * LANES, (j + 1) * LANES) for j in range(cols)]
    grids = ((f_hbm, stress), (c_hbm, fric), (m_hbm, mask))
    whole = [
        pltpu.make_async_copy(src, dst, sems.at[3 + k])
        for k, (src, dst) in enumerate(((ix_hbm, ixbuf), (w_hbm, wbuf)))
    ]

    @pl.when(sec_ref[0] == 0)
    def _():
        for q, (src, dst) in enumerate(grids):
            def one(e, carry, q=q, src=src, dst=dst):
                pltpu.make_async_copy(
                    src.at[pl.ds(src_ref[e], 1)], dst.at[pl.ds(e, 1)], sems.at[q]
                ).start()
                return carry

            lax.fori_loop(0, entries, one, 0, unroll=4)
        for copy in whole:
            copy.start()

    for p in range(partitions):
        rank[p] = 0
        at = p * block + CAP * cols
        outbox[at : at + SUB, :] = jnp.full((SUB, LANES), -1.0, F32)
        if zero_fill:
            outbox[p * block : at, :] = jnp.zeros((CAP * cols, LANES), F32)

    def assign(e, carry):
        target = tgt_ref[e]
        p = lax.div(target, height)
        k = rank[p]
        rank[p] = k + 1
        row = p * block
        slots[e] = row + k * cols
        label = jnp.full((1, LANES), target - p * height, jnp.int32).astype(F32)
        outbox[pl.ds(row + CAP * cols + k, 1), :] = label
        return carry

    lax.fori_loop(0, entries, assign, 0)

    @pl.when(sec_ref[0] == 0)
    def _():
        for q, (src, dst) in enumerate(grids):
            at = pl.ds(0, entries)
            pltpu.make_async_copy(src.at[at], dst.at[at], sems.at[q]).wait()
        for copy in whole:
            copy.wait()

        def group(g, carry):
            r = pl.ds(pl.multiple_of(g * SUB, SUB), SUB)
            table = [mask[r, s].astype(F32) * fric[r, s] * stress[r, s] for s in spans]
            for j, s in enumerate(spans):
                index = ixbuf[r, s]
                low, high = index & (LANES - 1), index >> 7
                got = [
                    jnp.take_along_axis(x, low, axis=1, mode="promise_in_bounds") for x in table
                ]
                bit = 1
                while len(got) > 1:
                    odd = (high & bit) != 0
                    got = [jnp.where(odd, got[t + 1], got[t]) for t in range(0, len(got), 2)]
                    bit *= 2
                sent[pl.ds(g * SUB * cols + j, SUB, stride=cols), :] = got[0] * wbuf[r, s]
            return carry

        lax.fori_loop(0, entries // SUB, group, 0)

        def place(e, carry):
            row = pl.multiple_of(slots[e], SUB)
            outbox[pl.ds(row, cols), :] = sent[pl.ds(pl.multiple_of(e * cols, cols), cols), :]
            return carry

        lax.fori_loop(0, entries, place, 0, unroll=4)

    @pl.when(sec_ref[0] == 1)
    def _():
        for p in range(partitions):
            outbox[p * block : p * block + CAP * cols, :] = jnp.zeros((CAP * cols, LANES), F32)


def melt_rows(section, source, destination, before, forcing, coefficient, mask, weights, index, partitions):
    entries, cells = weights.shape
    cols = cells // LANES
    return pl.pallas_call(
        functools.partial(melt_kernel, partitions * CAP != entries),
        out_shape=jax.ShapeDtypeStruct((partitions * (CAP * cols + SUB), LANES), F32),
        in_specs=[SMEM, SMEM, SMEM, ANY] + [HBM] * 5,
        out_specs=VMEM,
        scratch_shapes=[
            pltpu.VMEM((entries, cells), F32),
            pltpu.VMEM((entries, cells), F32),
            pltpu.VMEM((entries, cells), jnp.int32),
            pltpu.VMEM((entries, cells), F32),
            pltpu.VMEM((entries, cells), jnp.int32),
            pltpu.VMEM((entries * cols, LANES), F32),
            pltpu.SMEM((entries,), jnp.int32),
            pltpu.SMEM((partitions,), jnp.int32),
            pltpu.SemaphoreType.DMA((5,)),
        ],
        compiler_params=params(16),
        cost_estimate=cost(8),
        name="melt_rows",
    )(section, source, destination, before, *in_hbm(forcing, coefficient, mask, weights, index))


def tie_kernel(*refs):
    del refs


def tie(value, *before):
    return pl.pallas_call(
        tie_kernel,
        out_shape=jax.ShapeDtypeStruct(value.shape, value.dtype),
        in_specs=[ANY] * (1 + len(before)),
        out_specs=ANY,
        input_output_aliases={0: 0},
        compiler_params=params(1),
        cost_estimate=cost(0.1),
        name="tie",
    )(value, *before)


def sweep_tools(a_ref, b_ref, up_ref, down_ref):
    own, _, cells = a_ref.shape
    cols = cells // LANES
    spans = [slice(j * LANES, (j + 1) * LANES) for j in range(cols)]
    lane = lax.broadcasted_iota(jnp.int32, (SUB, LANES), 1)
    sub = lax.broadcasted_iota(jnp.int32, (SUB, LANES), 0)
    groups = ((0, DEEP), (DEEP, own), (DEEP + own, DEEP))

    def known(which, i, s):
        if i < DEEP:
            return up_ref[which * DEEP + i, :, s]
        if i < DEEP + own:
            return (a_ref, b_ref)[which][i - DEEP, :, s]
        return down_ref[which * DEEP + i - DEEP - own, :, s]

    low = cols >> BITS

    def sweep(old, store):
        def row(i):
            return [old(i, s) for s in spans]

        for k, (start, count) in enumerate(groups):
            north = [pltpu.roll(x, 1, 0) for x in row(start + count - 1)]
            if k > 0:
                north = [jnp.where(sub == 0, pltpu.roll(x, 1, 0), y) for x, y in zip(row(start - 1), north)]
            centre = row(start)
            for i in range(start, start + count):
                if i < start + count - 1:
                    south = row(i + 1)
                else:
                    south = [pltpu.roll(x, SUB - 1, 0) for x in row(start)]
                    if k < 2:
                        south = [
                            jnp.where(sub == SUB - 1, pltpu.roll(x, SUB - 1, 0), y)
                            for x, y in zip(row(i + 1), south)
                        ]
                west, east = sides(centre, lane, BITS)
                for first in range(low):
                    for j in range(first, cols, low):
                        s = spans[j]
                        around = (north[j] + south[j]) + 0.25 * (west[j] + east[j])
                        store(i, s, known(0, i, s) + known(1, i, s) * around)
                north, centre = centre, south

    def of(buf):
        return lambda i, s: buf[i, :, s]

    def into(buf):
        def store(i, s, x):
            buf[i, :, s] = x

        return store

    return spans, lane, sweep, lambda i, s: known(0, i, s), of, into


def ice_kernel(
    sec_ref, src_ref, tgt_ref, up_ref, down_ref, f_hbm, c_hbm, m_hbm, w_hbm,
    vel_hbm, flow_ref, gain_ref, slot_ref, list_ref,
    stress, fric, mask, wbuf, a_nat, b_nat, a_ref, b_ref, v_one, v_two, m_rows, v_rows, rank, filled, sems,
):
    height, cells = f_hbm.shape
    entries = w_hbm.shape[0]
    cols = cells // LANES
    partitions = rank.shape[0]
    rows = height // SUB
    chunks = 4
    size = height // chunks
    grids = ((f_hbm, stress), (c_hbm, fric), (m_hbm, mask))

    def part_copy(q, k):
        at = pl.ds(k * size, size)
        return pltpu.make_async_copy(grids[q][0].at[at], grids[q][1].at[at], sems.at[q * chunks + k])

    @pl.when(sec_ref[0] == 1)
    def _():
        for k in range(chunks):
            for q in range(3):
                part_copy(q, k).start()
        weight_copy = pltpu.make_async_copy(w_hbm, wbuf, sems.at[3 * chunks])
        weight_copy.start()
        for p in range(partitions):
            rank[p] = 0
        filled[0] = 0
        filled[1] = 0

        def assign(e, carry):
            target = tgt_ref[e]
            p = lax.div(target, height)
            k = rank[p]
            rank[p] = k + 1
            slot_ref[e] = p * CAP + k
            part = lax.div(k, 2)
            at = filled[part]
            filled[part] = at + 1
            list_ref[part * (entries // 2) + at] = e
            return carry

        lax.fori_loop(0, entries, assign, 0)
        spans, lane, sweep, start, of, into = sweep_tools(a_ref, b_ref, up_ref, down_ref)
        matrix = swap_matrix()
        for k in range(chunks):
            for q in range(3):
                part_copy(q, k).wait()
            r = slice(k * size, (k + 1) * size)
            b = [mask[r, s].astype(F32) / (2.5 + fric[r, s]) for s in spans]
            a = [x * stress[r, s] for x, s in zip(b, spans)]
            for nat, blocks in ((b_nat, b), (a_nat, a)):
                for j, x in enumerate(swap_bits(blocks, matrix)):
                    for t in range(k * (size // SUB), (k + 1) * (size // SUB)):
                        to = t * SUB
                        nat[j, to : to + SUB, :] = x[t * SUB - k * size : (t + 1) * SUB - k * size]
        for i in range(rows):
            r = pl.ds(i, SUB, stride=rows)
            for ref, nat in ((b_ref, b_nat), (a_ref, a_nat)):
                for j, s in enumerate(spans):
                    ref[i, :, s] = nat[j, r, :]

        def two(t, carry):
            sweep(of(v_one), into(v_two))
            sweep(of(v_two), into(v_one))
            return carry

        left = SWEEPS - 2
        sweep(start, into(v_one))
        lax.fori_loop(0, left // 2, two, 0)
        last = v_one
        if left % 2:
            sweep(of(v_one), into(v_two))
            last = v_two
        velocity = a_nat
        some = 8 if rows % 8 == 0 else rows
        for t in range(rows // some):
            at = slice(DEEP + t * some, DEEP + (t + 1) * some)
            blocks = [last[at, :, s].reshape(some * SUB, LANES) for s in spans]
            for j, x in enumerate(swap_bits(blocks, matrix)):
                for i in range(some):
                    velocity[j, pl.ds(t * some + i, SUB, stride=rows), :] = x[i * SUB : (i + 1) * SUB]
        outs = [
            pltpu.make_async_copy(velocity.at[j], vel_hbm.at[:, pl.ds(j * LANES, LANES)], sems.at[j])
            for j in range(cols)
        ]
        for out in outs:
            out.start()
        weight_copy.wait()

        def chosen(e, carry):
            at, r = pl.ds(e, 1), pl.ds(src_ref[e], 1)
            row = mask[r, :]
            for j, s in enumerate(spans):
                m_rows[j, at, :] = row[:, s]
                v_rows[j, at, :] = velocity[j, r, :]
            return carry

        lax.fori_loop(0, entries, chosen, 0, unroll=4)
        zero = jnp.zeros((SUB, LANES), F32)

        for g in range(entries // SUB):
            r = slice(g * SUB, (g + 1) * SUB)
            v = [v_rows[j, r, :] for j in range(cols)]
            ahead = [pltpu.roll(x, LANES - 1, 1) for x in v] + [zero]
            behind = [zero] + [pltpu.roll(x, 1, 1) for x in v]
            for j, s in enumerate(spans):
                east = jnp.where(lane == LANES - 1, ahead[j + 1], ahead[j])
                west = jnp.where(lane == 0, behind[j], behind[j + 1])
                gain = m_rows[j, r, :].astype(F32) * wbuf[r, s]
                gain_ref[r, s] = gain
                flow_ref[r, s] = gain * (-0.5 * (east - west))
        for out in outs:
            out.wait()


def ice_sweeps(section, source, destination, up, down, forcing, coefficient, mask, weights, partitions):
    height, cells = forcing.shape
    entries = weights.shape[0]
    cols = cells // LANES
    rows = height // SUB
    chosen = jax.ShapeDtypeStruct((entries, cells), F32)
    numbers = jax.ShapeDtypeStruct((entries,), jnp.int32)
    own = pltpu.VMEM((rows, SUB, cells), F32)
    spread = pltpu.VMEM((rows + 2 * DEEP, SUB, cells), F32)
    return pl.pallas_call(
        ice_kernel,
        out_shape=(
            jax.ShapeDtypeStruct((height, cells), F32), chosen, chosen,
            numbers, numbers,
        ),
        in_specs=[SMEM] * 3 + [VMEM] * 2 + [HBM] * 4,
        out_specs=(HBM, VMEM, VMEM, SMEM, SMEM),
        scratch_shapes=[
            pltpu.VMEM((height, cells), F32),
            pltpu.VMEM((height, cells), F32),
            pltpu.VMEM((height, cells), jnp.int32),
            pltpu.VMEM((entries, cells), F32),
            pltpu.VMEM((cols, height, LANES), F32),
            pltpu.VMEM((cols, height, LANES), F32),
            own, own, spread, spread,
            pltpu.VMEM((cols, entries, LANES), jnp.int32),
            pltpu.VMEM((cols, entries, LANES), F32),
            pltpu.SMEM((partitions,), jnp.int32),
            pltpu.SMEM((2,), jnp.int32),
            pltpu.SemaphoreType.DMA((max(3 * 4 + 1, cols),)),
        ],
        compiler_params=params(48),
        cost_estimate=cost(24),
        name="ice_sweeps",
    )(section, source, destination, up, down, *in_hbm(forcing, coefficient, mask, weights))


def label_columns(ref, block):
    partitions = ref.shape[0] // block
    return jnp.concatenate(
        [ref[pl.ds(block - SUB + k, partitions, stride=block), :] for k in range(CAP)], axis=0
    )


def row_table(refs, block, ranks, j, cols):
    return jnp.concatenate(
        [
            ref[pl.ds(k * cols + j, ref.shape[0] // block, stride=block), :]
            for ref in refs
            for k in range(ranks)
        ],
        axis=0,
    )


def values_kernel(sec_ref, handed_ref, source_ref, gain_ref, flow_ref, out_ref):
    entries, cells = gain_ref.shape
    cols = cells // LANES
    block = CAP * cols + SUB

    @pl.when(sec_ref[0] == 1)
    def _():
        labels = label_columns(handed_ref, block)[:, :entries]
        wanted = jnp.broadcast_to(source_ref[...].astype(F32), labels.shape)
        picker = jnp.transpose(jnp.where(labels == wanted, 1.0, 0.0)).astype(BF16)
        for j in range(cols):
            s = slice(j * LANES, (j + 1) * LANES)
            table = row_table((handed_ref,), block, CAP, j, cols)
            out_ref[:, s] = flow_ref[:, s] - gain_ref[:, s] * one_hot_dot(picker, table, 3)


def thickness_values(section, handed, source, gain, flow):
    return pl.pallas_call(
        values_kernel,
        out_shape=jax.ShapeDtypeStruct(gain.shape, F32),
        in_specs=[SMEM] + [VMEM] * 4,
        out_specs=VMEM,
        compiler_params=params(16),
        cost_estimate=cost(1),
        name="thickness_values",
    )(section, handed, source, gain, flow)


HIGH = 32
PACK = 4


def scatter_kernel(zero_fill, part, sec_ref, list_ref, slot_ref, v_ref, ix_ref, tile_ref, out_ref):
    entries, cells = v_ref.shape
    cols = cells // LANES
    count = entries // 2
    low_count = cells // HIGH
    across = LANES // low_count
    shift = low_count.bit_length() - 1
    block = 2 * cols if part else 2 * cols + SUB
    sent = CAP * cols + SUB
    unroll = 2 if count % (2 * PACK) == 0 else 1

    @pl.when(sec_ref[0] == 1)
    def _():
        partitions = out_ref.shape[0] // block
        if zero_fill:
            out_ref[...] = jnp.zeros_like(out_ref)
        if part == 0:
            for p in range(partitions):
                labels = tile_ref[p * sent + CAP * cols : (p + 1) * sent, :]
                out_ref[p * block + 2 * cols : (p + 1) * block, :] = labels
        high_row = lax.broadcasted_iota(jnp.int32, (HIGH, cells), 0).astype(BF16)
        low_row = lax.broadcasted_iota(jnp.int32, (low_count, cells), 0).astype(BF16)
        one, none = jnp.ones((low_count, cells), BF16), jnp.zeros((HIGH, cells), BF16)
        empty = jnp.zeros((low_count, cells), BF16)

        def operands(t):
            e = list_ref[part * count + t]
            slot = slot_ref[e]
            p = lax.div(slot, CAP)
            row = pl.multiple_of(p * block + (slot - p * CAP - 2 * part) * cols, SUB)
            v, index = v_ref[pl.ds(e, 1), :], ix_ref[pl.ds(e, 1), :]
            head = v.astype(BF16)
            rest = (v - head.astype(F32)).astype(BF16)
            upper = index >> shift
            upper = (upper & (across - 1)) * cols + (upper >> (across.bit_length() - 1))
            upper = upper.astype(F32).astype(BF16)
            lower = (index & (low_count - 1)).astype(F32).astype(BF16)
            here = jnp.broadcast_to(upper, (HIGH, cells)) == high_row
            left = [jnp.where(here, jnp.broadcast_to(x, (HIGH, cells)), none) for x in (head, rest)]
            right = jnp.where(jnp.broadcast_to(lower, (low_count, cells)) == low_row, one, empty)
            return row, left, right

        def some(t, carry):
            for u in range(unroll):
                rows, lefts, rights = zip(*[operands((t * unroll + u) * PACK + k) for k in range(PACK)])
                left = jnp.concatenate(sum(lefts, []), axis=0)
                right = jnp.concatenate(rights, axis=0)
                every = lax.dot_general(
                    left, right, (((1,), (1,)), ((), ())), preferred_element_type=F32
                )
                for k, row in enumerate(rows):
                    at = slice(k * low_count, (k + 1) * low_count)
                    top = 2 * k * HIGH
                    both = every[top : top + HIGH, at] + every[top + HIGH : top + 2 * HIGH, at]
                    out_ref[pl.ds(row, cols), :] = jnp.concatenate(
                        [both[h * cols : (h + 1) * cols] for h in range(across)], axis=1
                    )
            return carry

        lax.fori_loop(0, count // (unroll * PACK), some, 0)


def scatter_rows(part, section, lists, slot, values, index, tile, partitions):
    entries, cells = values.shape
    cols = cells // LANES
    block = 2 * cols if part else 2 * cols + SUB
    return pl.pallas_call(
        functools.partial(scatter_kernel, partitions * CAP != entries, part),
        out_shape=jax.ShapeDtypeStruct((partitions * block, LANES), F32),
        in_specs=[SMEM, SMEM, SMEM, VMEM, VMEM, ANY if part else VMEM],
        out_specs=VMEM,
        compiler_params=params(16),
        cost_estimate=cost(5),
        name="scatter_rows_%d" % part,
    )(section, lists, slot, values, index, tile)


def row_picker(labels, height):
    lane = lax.broadcasted_iota(jnp.int32, labels.shape, 1).astype(F32)
    picker = jnp.concatenate(
        [
            jnp.transpose(jnp.where(labels == lane + LANES * q, 1.0, 0.0))
            for q in range(height // LANES)
        ],
        axis=0,
    ).astype(BF16)
    return jnp.concatenate([picker] * 3, axis=1)


def own_place_kernel(sec_ref, own_ref, tile_ref, part_ref):
    cols, height, _ = part_ref.shape
    block = 2 * cols

    @pl.when(sec_ref[0] == 0)
    def _():
        labels = label_columns(tile_ref, block + SUB)
        picker = row_picker(labels[: labels.shape[0] // 2], height)
        for j in range(cols):
            table = jnp.concatenate(pieces(row_table((own_ref,), block, 2, j, cols), 3), axis=0)
            part_ref[j] = jnp.dot(picker, table, preferred_element_type=F32)


def own_place(section, own, tile, height, cells):
    return pl.pallas_call(
        own_place_kernel,
        out_shape=jax.ShapeDtypeStruct((cells // LANES, height, LANES), F32),
        in_specs=[SMEM, VMEM, VMEM],
        out_specs=VMEM,
        compiler_params=params(16),
        cost_estimate=cost(2),
        name="own_place",
    )(section, own, tile)


def place_kernel(sec_ref, tile_ref, handed_ref, part_ref, mask_ref, vel_hbm, out_hbm, result, sems):
    del vel_hbm
    cols, height, _ = part_ref.shape
    block = 2 * cols

    @pl.when(sec_ref[0] == 0)
    def _():
        labels = label_columns(tile_ref, block + SUB)
        picker = row_picker(labels[labels.shape[0] // 2 :], height)
        outs = []
        for j in range(cols):
            s = slice(j * LANES, (j + 1) * LANES)
            table = jnp.concatenate(pieces(row_table((handed_ref,), block, 2, j, cols), 3), axis=0)
            rows = part_ref[j] + jnp.dot(picker, table, preferred_element_type=F32)
            result[j] = mask_ref[:, s].astype(F32) * rows
            out = pltpu.make_async_copy(result.at[j], out_hbm.at[:, s], sems.at[j])
            out.start()
            outs.append(out)
        for out in outs:
            out.wait()


def place_rows(section, tile, handed, part, mask, velocity):
    height, cells = mask.shape
    cols = cells // LANES
    return pl.pallas_call(
        place_kernel,
        out_shape=jax.ShapeDtypeStruct((height, cells), F32),
        in_specs=[SMEM, VMEM, VMEM, VMEM, VMEM, HBM],
        out_specs=HBM,
        input_output_aliases={5: 0},
        scratch_shapes=[pltpu.VMEM((cols, height, LANES), F32), pltpu.SemaphoreType.DMA((cols,))],
        compiler_params=params(16),
        cost_estimate=cost(3),
        name="place_rows",
    )(section, tile, handed, part, mask, *in_hbm(velocity))


def per_device(forcing, coefficient, cell_mask, remap_weight, remap_index, link_source, link_target):
    partitions = lax.axis_size("dom")
    section = lax.axis_index("sect").astype(jnp.int32)
    flag = section.reshape(1)
    forcing, coefficient, mask = forcing[0], coefficient[0], cell_mask[0]
    weights, index = remap_weight[0], remap_index[0]
    source, destination = link_source.reshape(-1), link_target.reshape(-1)
    cells = forcing.shape[1]
    cols = cells // LANES

    both = ("sect", "dom")
    to_ice = [(i, partitions + i) for i in range(partitions)]
    to_ocean = [(partitions + i, i) for i in range(partitions)]
    onward = [(partitions + i, partitions + i + 1) for i in range(partitions - 1)]

    def exchange(x):
        return lax.all_to_all(x, "dom", 0, 0, tiled=True).reshape(-1, LANES)

    last, start = halo_rows(flag, forcing, coefficient, mask)
    up = lax.ppermute(last, both, onward)
    down = lax.ppermute(start, both, [(j, i) for i, j in onward])
    outbox = melt_rows(
        flag, source, destination, last, forcing, coefficient, mask, weights, index, partitions
    )
    arrived = exchange(tie(outbox, up, down).reshape(partitions, -1, LANES))
    velocity, flow, gain, slot, lists = ice_sweeps(
        flag, source, destination, up, down, forcing, coefficient, mask, weights, partitions
    )
    handed = lax.ppermute(tie(arrived, flow), both, to_ice)
    values = thickness_values(flag, handed, link_source, gain, flow)
    first = scatter_rows(0, flag, lists, slot, values, index, arrived, partitions)
    second = scatter_rows(1, flag, lists, slot, values, index, first, partitions)
    first = lax.ppermute(first, both, to_ocean)
    mine = first.reshape(partitions, -1, LANES)[:, : 2 * cols]
    arrived = exchange(jnp.where(section == 0, mine, second.reshape(partitions, -1, LANES)))
    handed = lax.ppermute(arrived, both, to_ocean)
    part = own_place(flag, arrived, first, *mask.shape)
    return place_rows(flag, first, handed, part, mask, velocity)[None]


def solution(mesh):
    in_specs = (P("sect", "dom", None),) * 5 + (P("sect", "dom"),) * 2
    return jax.shard_map(
        per_device, mesh=mesh, in_specs=in_specs, out_specs=P("sect", "dom", None), check_vma=False
    )
```

```python
import functools

import jax
import jax.numpy as jnp
from jax import lax
from jax.experimental import pallas as pl
from jax.experimental.pallas import tpu as pltpu
from jax.sharding import PartitionSpec as P

CAP = 4
SWEEPS = 20
LANES = 128
SUB = 8
HALO = 24
BITS = 2

F32 = jnp.float32
BF16 = jnp.bfloat16
ANY = pl.BlockSpec(memory_space=pl.ANY)
HBM = pl.BlockSpec(memory_space=pltpu.HBM)
VMEM = pl.BlockSpec(memory_space=pltpu.VMEM)
SMEM = pl.BlockSpec(memory_space=pltpu.SMEM)


def params(mib):
    return pltpu.CompilerParams(vmem_limit_bytes=mib * 2**20)


def in_hbm(*arrays):
    return [pltpu.with_memory_space_constraint(x, pltpu.HBM) for x in arrays]


def cost(microseconds):
    return pl.CostEstimate(flops=0, bytes_accessed=int(microseconds * 3.0e6), transcendentals=0)


def pieces(x, count):
    out = []
    for _ in range(count - 1):
        head = x.astype(BF16)
        out.append(head)
        x = x - head.astype(F32)
    out.append(x.astype(BF16))
    return out


def one_hot_dot(picker, table, count):
    total = None
    for piece in pieces(table, count):
        part = jnp.dot(picker, piece, preferred_element_type=F32)
        total = part if total is None else total + part
    return total


def swap_matrix():
    wide, low = LANES << BITS, (1 << BITS) - 1
    here = lax.broadcasted_iota(jnp.int32, (wide, wide), 0)
    there = lax.broadcasted_iota(jnp.int32, (wide, wide), 1)
    lane, group = here & (LANES - 1), here >> 7
    goal = (lane & low) * LANES + (lane - (lane & low)) + group
    return jnp.where(goal == there, 1.0, 0.0).astype(BF16)


def swap_bits(blocks, matrix):
    count, rows = len(blocks), blocks[0].shape[0]
    low = count >> BITS
    stacked = [[] for _ in range(3)]
    for j in range(low):
        x = jnp.concatenate(blocks[j::low], axis=1)
        for k in range(2):
            head = x.astype(BF16).astype(F32)
            stacked[k].append(head)
            x = x - head
        stacked[2].append(x)
    left = jnp.concatenate(sum(stacked, []), axis=0).astype(BF16)
    out = jnp.dot(left, matrix, preferred_element_type=F32)
    size = low * rows
    out = out[:size] + out[size : 2 * size] + out[2 * size :]
    return [
        out[j * rows : (j + 1) * rows, o * LANES : (o + 1) * LANES]
        for o in range(1 << BITS)
        for j in range(low)
    ]


def sides(c, lane, bits):
    count = len(c)
    low = count >> bits
    step = 1 << bits
    zero = jnp.zeros((SUB, LANES), F32)
    west, east = [None] * count, [None] * count
    for j in range(count):
        if j + low < count:
            east[j] = c[j + low]
            west[j + low] = c[j]
    ahead = [pltpu.roll(c[j], LANES - step, 1) for j in range(low)]
    ahead.append(jnp.where(lane == LANES - 1, zero, pltpu.roll(c[0], LANES - step - 1, 1)))
    behind = [jnp.where(lane == 0, zero, pltpu.roll(c[count - 1], step + 1, 1))]
    behind += [pltpu.roll(c[count - low + j], step, 1) for j in range(low)]
    for j in range(low):
        east[count - low + j] = jnp.where(lane < LANES - step, ahead[j], ahead[j + 1])
        west[j] = jnp.where(lane >= step, behind[j + 1], behind[j])
    return west, east


DEEP = HALO // SUB


def halo_kernel(sec_ref, f_hbm, c_hbm, m_hbm, last_ref, first_ref, stress, fric, mask, nat, sems):
    height, cells = f_hbm.shape
    cols = cells // LANES
    spans = [slice(j * LANES, (j + 1) * LANES) for j in range(cols)]

    @pl.when(sec_ref[0] == 1)
    def _():
        copies = []
        for k, start in enumerate((height - HALO, 0)):
            for src, dst in ((f_hbm, stress), (c_hbm, fric), (m_hbm, mask)):
                copy = pltpu.make_async_copy(src.at[pl.ds(start, HALO)], dst.at[k], sems.at[len(copies)])
                copy.start()
                copies.append(copy)
        matrix = swap_matrix()
        for copy in copies:
            copy.wait()
        for k, ref in enumerate((last_ref, first_ref)):
            b = [mask[k, :, s].astype(F32) / (2.5 + fric[k, :, s]) for s in spans]
            a = [x * stress[k, :, s] for x, s in zip(b, spans)]
            both = [jnp.concatenate([x, y], axis=0) for x, y in zip(a, b)]
            for j, x in enumerate(swap_bits(both, matrix)):
                nat[k, j] = x
            for q in range(2):
                for i in range(DEEP):
                    for j, s in enumerate(spans):
                        ref[q * DEEP + i, :, s] = nat[k, j, pl.ds(q * HALO + i, SUB, stride=DEEP), :]


def halo_rows(section, forcing, coefficient, mask):
    cells = forcing.shape[1]
    cols = cells // LANES
    out = jax.ShapeDtypeStruct((2 * DEEP, SUB, cells), F32)
    return pl.pallas_call(
        halo_kernel,
        out_shape=(out, out),
        in_specs=[SMEM, HBM, HBM, HBM],
        out_specs=(VMEM, VMEM),
        scratch_shapes=[
            pltpu.VMEM((2, HALO, cells), F32),
            pltpu.VMEM((2, HALO, cells), F32),
            pltpu.VMEM((2, HALO, cells), jnp.int32),
            pltpu.VMEM((2, cols, 2 * HALO, LANES), F32),
            pltpu.SemaphoreType.DMA((6,)),
        ],
        compiler_params=params(16),
        cost_estimate=cost(2),
        name="halo_rows",
    )(section, *in_hbm(forcing, coefficient, mask))


def melt_kernel(
    zero_fill, sec_ref, src_ref, tgt_ref, tie_ref, f_hbm, c_hbm, m_hbm, w_hbm, ix_hbm,
    outbox, stress, fric, mask, wbuf, ixbuf, sent, slots, rank, sems,
):
    del tie_ref
    height = f_hbm.shape[0]
    entries, cells = w_hbm.shape
    cols = cells // LANES
    block = CAP * cols + SUB
    partitions = rank.shape[0]
    spans = [slice(j * LANES, (j + 1) * LANES) for j in range(cols)]
    grids = ((f_hbm, stress), (c_hbm, fric), (m_hbm, mask))
    whole = [
        pltpu.make_async_copy(src, dst, sems.at[3 + k])
        for k, (src, dst) in enumerate(((ix_hbm, ixbuf), (w_hbm, wbuf)))
    ]

    @pl.when(sec_ref[0] == 0)
    def _():
        for q, (src, dst) in enumerate(grids):
            def one(e, carry, q=q, src=src, dst=dst):
                pltpu.make_async_copy(
                    src.at[pl.ds(src_ref[e], 1)], dst.at[pl.ds(e, 1)], sems.at[q]
                ).start()
                return carry

            lax.fori_loop(0, entries, one, 0, unroll=4)
        for copy in whole:
            copy.start()

    for p in range(partitions):
        rank[p] = 0
        at = p * block + CAP * cols
        outbox[at : at + SUB, :] = jnp.full((SUB, LANES), -1.0, F32)
        if zero_fill:
            outbox[p * block : at, :] = jnp.zeros((CAP * cols, LANES), F32)

    def assign(e, carry):
        target = tgt_ref[e]
        p = lax.div(target, height)
        k = rank[p]
        rank[p] = k + 1
        row = p * block
        slots[e] = row + k * cols
        label = jnp.full((1, LANES), target - p * height, jnp.int32).astype(F32)
        outbox[pl.ds(row + CAP * cols + k, 1), :] = label
        return carry

    lax.fori_loop(0, entries, assign, 0)

    @pl.when(sec_ref[0] == 0)
    def _():
        for q, (src, dst) in enumerate(grids):
            at = pl.ds(0, entries)
            pltpu.make_async_copy(src.at[at], dst.at[at], sems.at[q]).wait()
        for copy in whole:
            copy.wait()

        def group(g, carry):
            r = pl.ds(pl.multiple_of(g * SUB, SUB), SUB)
            table = [mask[r, s].astype(F32) * fric[r, s] * stress[r, s] for s in spans]
            for j, s in enumerate(spans):
                index = ixbuf[r, s]
                low, high = index & (LANES - 1), index >> 7
                got = [
                    jnp.take_along_axis(x, low, axis=1, mode="promise_in_bounds") for x in table
                ]
                bit = 1
                while len(got) > 1:
                    odd = (high & bit) != 0
                    got = [jnp.where(odd, got[t + 1], got[t]) for t in range(0, len(got), 2)]
                    bit *= 2
                sent[pl.ds(g * SUB * cols + j, SUB, stride=cols), :] = got[0] * wbuf[r, s]
            return carry

        lax.fori_loop(0, entries // SUB, group, 0)

        def place(e, carry):
            row = pl.multiple_of(slots[e], SUB)
            outbox[pl.ds(row, cols), :] = sent[pl.ds(pl.multiple_of(e * cols, cols), cols), :]
            return carry

        lax.fori_loop(0, entries, place, 0, unroll=4)

    @pl.when(sec_ref[0] == 1)
    def _():
        for p in range(partitions):
            outbox[p * block : p * block + CAP * cols, :] = jnp.zeros((CAP * cols, LANES), F32)


def melt_rows(section, source, destination, before, forcing, coefficient, mask, weights, index, partitions):
    entries, cells = weights.shape
    cols = cells // LANES
    return pl.pallas_call(
        functools.partial(melt_kernel, partitions * CAP != entries),
        out_shape=jax.ShapeDtypeStruct((partitions * (CAP * cols + SUB), LANES), F32),
        in_specs=[SMEM, SMEM, SMEM, ANY] + [HBM] * 5,
        out_specs=VMEM,
        scratch_shapes=[
            pltpu.VMEM((entries, cells), F32),
            pltpu.VMEM((entries, cells), F32),
            pltpu.VMEM((entries, cells), jnp.int32),
            pltpu.VMEM((entries, cells), F32),
            pltpu.VMEM((entries, cells), jnp.int32),
            pltpu.VMEM((entries * cols, LANES), F32),
            pltpu.SMEM((entries,), jnp.int32),
            pltpu.SMEM((partitions,), jnp.int32),
            pltpu.SemaphoreType.DMA((5,)),
        ],
        compiler_params=params(16),
        cost_estimate=cost(8),
        name="melt_rows",
    )(section, source, destination, before, *in_hbm(forcing, coefficient, mask, weights, index))


def tie_kernel(*refs):
    del refs


def tie(value, *before):
    return pl.pallas_call(
        tie_kernel,
        out_shape=jax.ShapeDtypeStruct(value.shape, value.dtype),
        in_specs=[ANY] * (1 + len(before)),
        out_specs=ANY,
        input_output_aliases={0: 0},
        compiler_params=params(1),
        cost_estimate=cost(0.1),
        name="tie",
    )(value, *before)


def sweep_tools(a_ref, b_ref, up_ref, down_ref):
    own, _, cells = a_ref.shape
    cols = cells // LANES
    spans = [slice(j * LANES, (j + 1) * LANES) for j in range(cols)]
    lane = lax.broadcasted_iota(jnp.int32, (SUB, LANES), 1)
    sub = lax.broadcasted_iota(jnp.int32, (SUB, LANES), 0)
    groups = ((0, DEEP), (DEEP, own), (DEEP + own, DEEP))

    def known(which, i, s):
        if i < DEEP:
            return up_ref[which * DEEP + i, :, s]
        if i < DEEP + own:
            return (a_ref, b_ref)[which][i - DEEP, :, s]
        return down_ref[which * DEEP + i - DEEP - own, :, s]

    low = cols >> BITS

    def sweep(old, store, last=False):
        def row(i):
            return [old(i, s) for s in spans]

        for k, (start, count) in enumerate(groups):
            if last and k != 1:
                continue
            north = [pltpu.roll(x, 1, 0) for x in row(start + count - 1)]
            if k > 0:
                north = [jnp.where(sub == 0, pltpu.roll(x, 1, 0), y) for x, y in zip(row(start - 1), north)]
            centre = row(start)
            for i in range(start, start + count):
                if i < start + count - 1:
                    south = row(i + 1)
                else:
                    south = [pltpu.roll(x, SUB - 1, 0) for x in row(start)]
                    if k < 2:
                        south = [
                            jnp.where(sub == SUB - 1, pltpu.roll(x, SUB - 1, 0), y)
                            for x, y in zip(row(i + 1), south)
                        ]
                west, east = sides(centre, lane, BITS)
                for first in range(low):
                    for j in range(first, cols, low):
                        s = spans[j]
                        around = (north[j] + south[j]) + 0.25 * (west[j] + east[j])
                        store(i, s, known(0, i, s) + known(1, i, s) * around)
                north, centre = centre, south

    def of(buf):
        return lambda i, s: buf[i, :, s]

    def into(buf):
        def store(i, s, x):
            buf[i, :, s] = x

        return store

    return spans, lane, sweep, lambda i, s: known(0, i, s), of, into


def ice_kernel(
    sec_ref, src_ref, tgt_ref, up_ref, down_ref, f_hbm, c_hbm, m_hbm, w_hbm,
    vel_hbm, flow_ref, gain_ref, slot_ref, list_ref,
    stress, fric, mask, wbuf, a_nat, b_nat, a_ref, b_ref, v_one, v_two, m_rows, v_rows, rank, filled, sems,
):
    height, cells = f_hbm.shape
    entries = w_hbm.shape[0]
    cols = cells // LANES
    partitions = rank.shape[0]
    rows = height // SUB
    chunks = 4
    size = height // chunks
    grids = ((f_hbm, stress), (c_hbm, fric), (m_hbm, mask))

    def part_copy(q, k):
        at = pl.ds(k * size, size)
        return pltpu.make_async_copy(grids[q][0].at[at], grids[q][1].at[at], sems.at[q * chunks + k])

    @pl.when(sec_ref[0] == 1)
    def _():
        for k in range(chunks):
            for q in range(3):
                part_copy(q, k).start()
        weight_copy = pltpu.make_async_copy(w_hbm, wbuf, sems.at[3 * chunks])
        weight_copy.start()
        for p in range(partitions):
            rank[p] = 0
        filled[0] = 0
        filled[1] = 0

        def assign(e, carry):
            target = tgt_ref[e]
            p = lax.div(target, height)
            k = rank[p]
            rank[p] = k + 1
            slot_ref[e] = p * CAP + k
            part = lax.div(k, 2)
            at = filled[part]
            filled[part] = at + 1
            list_ref[part * (entries // 2) + at] = e
            return carry

        lax.fori_loop(0, entries, assign, 0)
        spans, lane, sweep, start, of, into = sweep_tools(a_ref, b_ref, up_ref, down_ref)
        matrix = swap_matrix()
        for k in range(chunks):
            for q in range(3):
                part_copy(q, k).wait()
            r = slice(k * size, (k + 1) * size)
            b = [mask[r, s].astype(F32) / (2.5 + fric[r, s]) for s in spans]
            a = [x * stress[r, s] for x, s in zip(b, spans)]
            for nat, blocks in ((b_nat, b), (a_nat, a)):
                for j, x in enumerate(swap_bits(blocks, matrix)):
                    for t in range(k * (size // SUB), (k + 1) * (size // SUB)):
                        to = t * SUB
                        nat[j, to : to + SUB, :] = x[t * SUB - k * size : (t + 1) * SUB - k * size]
        for i in range(rows):
            r = pl.ds(i, SUB, stride=rows)
            for ref, nat in ((b_ref, b_nat), (a_ref, a_nat)):
                for j, s in enumerate(spans):
                    ref[i, :, s] = nat[j, r, :]

        def two(t, carry):
            sweep(of(v_one), into(v_two))
            sweep(of(v_two), into(v_one))
            return carry

        left = SWEEPS - 3
        sweep(start, into(v_one))
        lax.fori_loop(0, left // 2, two, 0)
        before, last = v_one, v_two
        if left % 2:
            sweep(of(v_one), into(v_two))
            before, last = v_two, v_one
        sweep(of(before), into(last), last=True)
        velocity = a_nat
        some = 8 if rows % 8 == 0 else rows
        for t in range(rows // some):
            at = slice(DEEP + t * some, DEEP + (t + 1) * some)
            blocks = [last[at, :, s].reshape(some * SUB, LANES) for s in spans]
            for j, x in enumerate(swap_bits(blocks, matrix)):
                for i in range(some):
                    velocity[j, pl.ds(t * some + i, SUB, stride=rows), :] = x[i * SUB : (i + 1) * SUB]
        outs = [
            pltpu.make_async_copy(velocity.at[j], vel_hbm.at[:, pl.ds(j * LANES, LANES)], sems.at[j])
            for j in range(cols)
        ]
        for out in outs:
            out.start()
        weight_copy.wait()

        def chosen(e, carry):
            at, r = pl.ds(e, 1), pl.ds(src_ref[e], 1)
            row = mask[r, :]
            for j, s in enumerate(spans):
                m_rows[j, at, :] = row[:, s]
                v_rows[j, at, :] = velocity[j, r, :]
            return carry

        lax.fori_loop(0, entries, chosen, 0, unroll=4)
        zero = jnp.zeros((SUB, LANES), F32)

        for g in range(entries // SUB):
            r = slice(g * SUB, (g + 1) * SUB)
            v = [v_rows[j, r, :] for j in range(cols)]
            ahead = [pltpu.roll(x, LANES - 1, 1) for x in v] + [zero]
            behind = [zero] + [pltpu.roll(x, 1, 1) for x in v]
            for j, s in enumerate(spans):
                east = jnp.where(lane == LANES - 1, ahead[j + 1], ahead[j])
                west = jnp.where(lane == 0, behind[j], behind[j + 1])
                gain = m_rows[j, r, :].astype(F32) * wbuf[r, s]
                gain_ref[r, s] = gain
                flow_ref[r, s] = gain * (-0.5 * (east - west))
        for out in outs:
            out.wait()


def ice_sweeps(section, source, destination, up, down, forcing, coefficient, mask, weights, partitions):
    height, cells = forcing.shape
    entries = weights.shape[0]
    cols = cells // LANES
    rows = height // SUB
    chosen = jax.ShapeDtypeStruct((entries, cells), F32)
    numbers = jax.ShapeDtypeStruct((entries,), jnp.int32)
    own = pltpu.VMEM((rows, SUB, cells), F32)
    spread = pltpu.VMEM((rows + 2 * DEEP, SUB, cells), F32)
    return pl.pallas_call(
        ice_kernel,
        out_shape=(
            jax.ShapeDtypeStruct((height, cells), F32), chosen, chosen,
            numbers, numbers,
        ),
        in_specs=[SMEM] * 3 + [VMEM] * 2 + [HBM] * 4,
        out_specs=(HBM, VMEM, VMEM, SMEM, SMEM),
        scratch_shapes=[
            pltpu.VMEM((height, cells), F32),
            pltpu.VMEM((height, cells), F32),
            pltpu.VMEM((height, cells), jnp.int32),
            pltpu.VMEM((entries, cells), F32),
            pltpu.VMEM((cols, height, LANES), F32),
            pltpu.VMEM((cols, height, LANES), F32),
            own, own, spread, spread,
            pltpu.VMEM((cols, entries, LANES), jnp.int32),
            pltpu.VMEM((cols, entries, LANES), F32),
            pltpu.SMEM((partitions,), jnp.int32),
            pltpu.SMEM((2,), jnp.int32),
            pltpu.SemaphoreType.DMA((max(3 * 4 + 1, cols),)),
        ],
        compiler_params=params(48),
        cost_estimate=cost(24),
        name="ice_sweeps",
    )(section, source, destination, up, down, *in_hbm(forcing, coefficient, mask, weights))


def label_columns(ref, block):
    partitions = ref.shape[0] // block
    return jnp.concatenate(
        [ref[pl.ds(block - SUB + k, partitions, stride=block), :] for k in range(CAP)], axis=0
    )


def row_table(refs, block, ranks, j, cols):
    return jnp.concatenate(
        [
            ref[pl.ds(k * cols + j, ref.shape[0] // block, stride=block), :]
            for ref in refs
            for k in range(ranks)
        ],
        axis=0,
    )


def values_kernel(sec_ref, handed_ref, source_ref, gain_ref, flow_ref, out_ref):
    entries, cells = gain_ref.shape
    cols = cells // LANES
    block = CAP * cols + SUB

    @pl.when(sec_ref[0] == 1)
    def _():
        labels = label_columns(handed_ref, block)[:, :entries]
        wanted = jnp.broadcast_to(source_ref[...].astype(F32), labels.shape)
        picker = jnp.transpose(jnp.where(labels == wanted, 1.0, 0.0)).astype(BF16)
        for j in range(cols):
            s = slice(j * LANES, (j + 1) * LANES)
            table = row_table((handed_ref,), block, CAP, j, cols)
            out_ref[:, s] = flow_ref[:, s] - gain_ref[:, s] * one_hot_dot(picker, table, 3)


def thickness_values(section, handed, source, gain, flow):
    return pl.pallas_call(
        values_kernel,
        out_shape=jax.ShapeDtypeStruct(gain.shape, F32),
        in_specs=[SMEM] + [VMEM] * 4,
        out_specs=VMEM,
        compiler_params=params(16),
        cost_estimate=cost(1),
        name="thickness_values",
    )(section, handed, source, gain, flow)


HIGH = 32
PACK = 4


def scatter_kernel(zero_fill, part, sec_ref, list_ref, slot_ref, v_ref, ix_ref, tile_ref, out_ref):
    entries, cells = v_ref.shape
    cols = cells // LANES
    count = entries // 2
    low_count = cells // HIGH
    across = LANES // low_count
    shift = low_count.bit_length() - 1
    block = 2 * cols if part else 2 * cols + SUB
    sent = CAP * cols + SUB
    unroll = 4 if count % (4 * PACK) == 0 else 1

    @pl.when(sec_ref[0] == 1)
    def _():
        partitions = out_ref.shape[0] // block
        if zero_fill:
            out_ref[...] = jnp.zeros_like(out_ref)
        if part == 0:
            for p in range(partitions):
                labels = tile_ref[p * sent + CAP * cols : (p + 1) * sent, :]
                out_ref[p * block + 2 * cols : (p + 1) * block, :] = labels
        high_row = lax.broadcasted_iota(jnp.int32, (HIGH, cells), 0).astype(BF16)
        low_row = lax.broadcasted_iota(jnp.int32, (low_count, cells), 0).astype(BF16)
        one, none = jnp.ones((low_count, cells), BF16), jnp.zeros((HIGH, cells), BF16)
        empty = jnp.zeros((low_count, cells), BF16)

        def operands(t):
            e = list_ref[part * count + t]
            slot = slot_ref[e]
            p = lax.div(slot, CAP)
            row = pl.multiple_of(p * block + (slot - p * CAP - 2 * part) * cols, SUB)
            v, index = v_ref[pl.ds(e, 1), :], ix_ref[pl.ds(e, 1), :]
            head = v.astype(BF16)
            rest = (v - head.astype(F32)).astype(BF16)
            upper = index >> shift
            upper = (upper & (across - 1)) * cols + (upper >> (across.bit_length() - 1))
            upper = upper.astype(F32).astype(BF16)
            lower = (index & (low_count - 1)).astype(F32).astype(BF16)
            here = jnp.broadcast_to(upper, (HIGH, cells)) == high_row
            left = [jnp.where(here, jnp.broadcast_to(x, (HIGH, cells)), none) for x in (head, rest)]
            right = jnp.where(jnp.broadcast_to(lower, (low_count, cells)) == low_row, one, empty)
            return row, left, right

        def some(t, carry):
            for u in range(unroll):
                rows, lefts, rights = zip(*[operands((t * unroll + u) * PACK + k) for k in range(PACK)])
                left = jnp.concatenate(sum(lefts, []), axis=0)
                right = jnp.concatenate(rights, axis=0)
                every = lax.dot_general(
                    left, right, (((1,), (1,)), ((), ())), preferred_element_type=F32
                )
                for k, row in enumerate(rows):
                    at = slice(k * low_count, (k + 1) * low_count)
                    top = 2 * k * HIGH
                    both = every[top : top + HIGH, at] + every[top + HIGH : top + 2 * HIGH, at]
                    out_ref[pl.ds(row, cols), :] = jnp.concatenate(
                        [both[h * cols : (h + 1) * cols] for h in range(across)], axis=1
                    )
            return carry

        lax.fori_loop(0, count // (unroll * PACK), some, 0)


def scatter_rows(part, section, lists, slot, values, index, tile, partitions):
    entries, cells = values.shape
    cols = cells // LANES
    block = 2 * cols if part else 2 * cols + SUB
    return pl.pallas_call(
        functools.partial(scatter_kernel, partitions * CAP != entries, part),
        out_shape=jax.ShapeDtypeStruct((partitions * block, LANES), F32),
        in_specs=[SMEM, SMEM, SMEM, VMEM, VMEM, ANY if part else VMEM],
        out_specs=VMEM,
        compiler_params=params(16),
        cost_estimate=cost(5),
        name="scatter_rows_%d" % part,
    )(section, lists, slot, values, index, tile)


def row_picker(labels, height):
    lane = lax.broadcasted_iota(jnp.int32, labels.shape, 1).astype(F32)
    picker = jnp.concatenate(
        [
            jnp.transpose(jnp.where(labels == lane + LANES * q, 1.0, 0.0))
            for q in range(height // LANES)
        ],
        axis=0,
    ).astype(BF16)
    return jnp.concatenate([picker] * 3, axis=1)


def own_place_kernel(sec_ref, own_ref, tile_ref, part_ref):
    cols, height, _ = part_ref.shape
    block = 2 * cols

    @pl.when(sec_ref[0] == 0)
    def _():
        labels = label_columns(tile_ref, block + SUB)
        picker = row_picker(labels[: labels.shape[0] // 2], height)
        for j in range(cols):
            table = jnp.concatenate(pieces(row_table((own_ref,), block, 2, j, cols), 3), axis=0)
            part_ref[j] = jnp.dot(picker, table, preferred_element_type=F32)


def own_place(section, own, tile, height, cells):
    return pl.pallas_call(
        own_place_kernel,
        out_shape=jax.ShapeDtypeStruct((cells // LANES, height, LANES), F32),
        in_specs=[SMEM, VMEM, VMEM],
        out_specs=VMEM,
        compiler_params=params(16),
        cost_estimate=cost(2),
        name="own_place",
    )(section, own, tile)


def place_kernel(sec_ref, tile_ref, handed_ref, part_ref, mask_ref, vel_hbm, out_hbm, result, sems):
    del vel_hbm
    cols, height, _ = part_ref.shape
    block = 2 * cols

    @pl.when(sec_ref[0] == 0)
    def _():
        labels = label_columns(tile_ref, block + SUB)
        picker = row_picker(labels[labels.shape[0] // 2 :], height)
        outs = []
        for j in range(cols):
            s = slice(j * LANES, (j + 1) * LANES)
            table = jnp.concatenate(pieces(row_table((handed_ref,), block, 2, j, cols), 3), axis=0)
            rows = part_ref[j] + jnp.dot(picker, table, preferred_element_type=F32)
            result[j] = mask_ref[:, s].astype(F32) * rows
            out = pltpu.make_async_copy(result.at[j], out_hbm.at[:, s], sems.at[j])
            out.start()
            outs.append(out)
        for out in outs:
            out.wait()


def place_rows(section, tile, handed, part, mask, velocity):
    height, cells = mask.shape
    cols = cells // LANES
    return pl.pallas_call(
        place_kernel,
        out_shape=jax.ShapeDtypeStruct((height, cells), F32),
        in_specs=[SMEM, VMEM, VMEM, VMEM, VMEM, HBM],
        out_specs=HBM,
        input_output_aliases={5: 0},
        scratch_shapes=[pltpu.VMEM((cols, height, LANES), F32), pltpu.SemaphoreType.DMA((cols,))],
        compiler_params=params(16),
        cost_estimate=cost(3),
        name="place_rows",
    )(section, tile, handed, part, mask, *in_hbm(velocity))


def per_device(forcing, coefficient, cell_mask, remap_weight, remap_index, link_source, link_target):
    partitions = lax.axis_size("dom")
    section = lax.axis_index("sect").astype(jnp.int32)
    flag = section.reshape(1)
    forcing, coefficient, mask = forcing[0], coefficient[0], cell_mask[0]
    weights, index = remap_weight[0], remap_index[0]
    source, destination = link_source.reshape(-1), link_target.reshape(-1)
    cells = forcing.shape[1]
    cols = cells // LANES

    both = ("sect", "dom")
    to_ice = [(i, partitions + i) for i in range(partitions)]
    to_ocean = [(partitions + i, i) for i in range(partitions)]
    onward = [(partitions + i, partitions + i + 1) for i in range(partitions - 1)]

    def exchange(x):
        return lax.all_to_all(x, "dom", 0, 0, tiled=True).reshape(-1, LANES)

    last, start = halo_rows(flag, forcing, coefficient, mask)
    up = lax.ppermute(last, both, onward)
    down = lax.ppermute(start, both, [(j, i) for i, j in onward])
    outbox = melt_rows(
        flag, source, destination, last, forcing, coefficient, mask, weights, index, partitions
    )
    arrived = exchange(tie(outbox, up, down).reshape(partitions, -1, LANES))
    velocity, flow, gain, slot, lists = ice_sweeps(
        flag, source, destination, up, down, forcing, coefficient, mask, weights, partitions
    )
    handed = lax.ppermute(tie(arrived, flow), both, to_ice)
    values = thickness_values(flag, handed, link_source, gain, flow)
    first = scatter_rows(0, flag, lists, slot, values, index, arrived, partitions)
    second = scatter_rows(1, flag, lists, slot, values, index, first, partitions)
    first = lax.ppermute(first, both, to_ocean)
    mine = first.reshape(partitions, -1, LANES)[:, : 2 * cols]
    arrived = exchange(jnp.where(section == 0, mine, second.reshape(partitions, -1, LANES)))
    handed = lax.ppermute(arrived, both, to_ocean)
    part = own_place(flag, arrived, first, *mask.shape)
    return place_rows(flag, first, handed, part, mask, velocity)[None]


def solution(mesh):
    in_specs = (P("sect", "dom", None),) * 5 + (P("sect", "dom"),) * 2
    return jax.shard_map(
        per_device, mesh=mesh, in_specs=in_specs, out_specs=P("sect", "dom", None), check_vma=False
    )
```
